32 devices in a mesh: dp: 16 (over z, y, x), tensor: 2 (over core).
Axes of the slice: x: 2, y: 2, z: 4, core: 2. Of those that a mesh axis runs over, the one named last changes fastest.
Arguments:
- layer_input: bfloat16 [16384, 768], P('dp'), may hold values from -6 to 6
- cotangent: bfloat16 [16384, 768], P('dp'), may hold values from -6 to 6
- segment_ids: int32 [16384], P('dp'), may hold values from -1 to 1, as said below
- attend_weight: float32 [768, 2304], P('dp', 'tensor'), may hold values from -0.21875 to 0.21875
- output_weight: float32 [768, 768], P('dp', 'tensor'), may hold values from -1.25 to 1.25
- widen_weight: float32 [768, 3072], P('dp', 'tensor'), may hold values from -0.21875 to 0.21875
- narrow_weight: float32 [768, 3072], P('dp', 'tensor'), may hold values from -0.109375 to 0.109375
- attend_moment: float32 [768, 2304], P('dp', 'tensor')
- output_moment: float32 [768, 768], P('dp', 'tensor')
- widen_moment: float32 [768, 3072], P('dp', 'tensor')
- narrow_moment: float32 [768, 3072], P('dp', 'tensor')
- vector_params: float32 [13, 768], replicated
- vector_first: float32 [13, 768], replicated
- vector_second: float32 [13, 768], replicated, as said below
Outputs:
- block_output: bfloat16 [16384, 768], P('dp', 'tensor')
- input_grad: float32 [16384, 768], P('dp')
- attend_grad: float32 [768, 2304], P('dp', 'tensor')
- output_grad: float32 [768, 768], P('dp', 'tensor')
- widen_grad: float32 [768, 3072], P('dp', 'tensor')
- narrow_grad: float32 [768, 3072], P('dp', 'tensor')
- momentum_attend: float32 [768, 2304], P('dp', 'tensor')
- momentum_output: float32 [768, 768], P('dp', 'tensor')
- momentum_widen: float32 [768, 3072], P('dp', 'tensor')
- momentum_narrow: float32 [768, 3072], P('dp', 'tensor')
- updated_attend: float32 [768, 2304], P('dp', 'tensor')
- updated_output: float32 [768, 768], P('dp', 'tensor')
- updated_widen: float32 [768, 3072], P('dp', 'tensor')
- updated_narrow: float32 [768, 3072], P('dp', 'tensor')
- vector_grad: float32 [13, 768], replicated
- first_moment: float32 [13, 768], replicated
- second_moment: float32 [13, 768], replicated
- updated_vectors: float32 [13, 768], replicated
The draws below stay inside these ranges and needn't reach their ends.
Inputs may be any that keep to these rules, and one draw needn't show every extreme that they name: `segment_ids`: in each group of 1024 slots the ids are 0 and possibly then 1 over a live prefix of one or more blocks of 512 slots (the last possibly partly filled), followed by -1; id 0 covers 512 // 2 slots or more; in every draw some group is one sequence of all 1024 slots. `vector_second`: entries are positive.
All inputs are finite; a program needn't handle non-finite values.
Results may differ from the reference program's by a relative error of at most 0.009.
The reference program's roundings to bfloat16 on the way count: a program that leaves them out, or rounds other values in their place, can miss the bound.
Values may be sent and summed in bfloat16 or wider, within the bound.
No kernel may reach another device: no remote copies, remote signals or barrier semaphores. Data moves between devices by JAX's collectives and lax.ppermute only.
A program may use at most 192 MiB of HBM per device.

```python
import math
import jax
import jax.numpy as jnp
from jax import lax

D = 768
HEADS = 12
HEAD_DIM = 64
FF = 3072
ROTARY = 16
BLOCK = 512
BLOCKS_DEV = 2
NS_STEPS = 5
STEP = 10
DEV_TOK = 1024
TOKENS = 16384
VEC_ROWS = 13


def draw_segment_ids(key, part):
    key = jax.random.fold_in(key, 11)
    block_key, pad_key, cut_key, full_key = jax.random.split(key, 4)
    devices = TOKENS // DEV_TOK
    live_blocks = jax.random.randint(block_key, (devices,), 1, BLOCKS_DEV + 1)
    padding = jax.random.randint(pad_key, (devices,), 0, BLOCK // 2)
    cut_points = jax.random.randint(cut_key, (devices,), BLOCK // 2, DEV_TOK + 1)
    full_device = jax.random.randint(full_key, (), 0, devices)
    onehot = jnp.arange(devices, dtype=jnp.int32) == full_device
    live_blocks = jnp.where(onehot, BLOCKS_DEV, live_blocks)
    padding = jnp.where(onehot, 0, padding)
    cut_points = jnp.where(onehot, DEV_TOK, cut_points)
    live_count = live_blocks * BLOCK - padding
    token_index = jnp.arange(DEV_TOK, dtype=jnp.int32)
    second = (token_index[None, :] >= cut_points[:, None]).astype(jnp.int32)
    segments = jnp.where(token_index[None, :] < live_count[:, None], second, -1)
    return segments.reshape(-1).astype(jnp.int32)


def moment_draw(key, row_count, column_count, factor):
    return factor * math.sqrt(TOKENS) * jax.random.normal(key, (row_count, column_count), jnp.float32)


def draw_attend_moment(key, part):
    key = jax.random.fold_in(key, 21)
    return moment_draw(key, D, 3 * D, 0.1)


def draw_output_moment(key, part):
    key = jax.random.fold_in(key, 22)
    return moment_draw(key, D, D, 0.1)


def draw_widen_moment(key, part):
    key = jax.random.fold_in(key, 23)
    return moment_draw(key, D, FF, 0.2)


def draw_narrow_moment(key, part):
    key = jax.random.fold_in(key, 24)
    return moment_draw(key, D, FF, 0.4)


def draw_vector_params(key, part):
    key = jax.random.fold_in(key, 31)
    gain_key, shift_key = jax.random.split(key)
    gains = jax.random.uniform(gain_key, (VEC_ROWS, D), jnp.float32, 0.6, 1.4)
    shifts = 0.2 * jnp.clip(jax.random.normal(shift_key, (VEC_ROWS, D), jnp.float32), -4.0, 4.0)
    row_index = jnp.arange(VEC_ROWS, dtype=jnp.int32)
    is_gain = (row_index == 0) | (row_index == 2)
    return jnp.where(is_gain[:, None], gains, shifts)


def draw_vector_first(key, part):
    key = jax.random.fold_in(key, 32)
    return 0.03 * math.sqrt(TOKENS) * jnp.clip(jax.random.normal(key, (VEC_ROWS, D), jnp.float32), -4.0, 4.0)


def draw_vector_second(key, part):
    key = jax.random.fold_in(key, 33)
    spread = jax.random.uniform(key, (VEC_ROWS, D), jnp.float32, math.log(0.005), math.log(0.05))
    return TOKENS * jnp.exp(spread)


def shard_levels(rng, extent, cuts, least, largest):
    def one(axis_at, parts):
        draws = jax.random.uniform(jax.random.fold_in(jax.random.fold_in(rng, 6), axis_at), (parts,), jnp.float32, least / len(cuts), largest / len(cuts))
        return jnp.repeat(jnp.exp(draws), extent[axis_at] // parts).reshape((-1,) + (1,) * (len(extent) - axis_at - 1))

    loudness = one(*cuts[0])
    for cut in cuts[1:]:
        loudness = loudness * one(*cut)
    return loudness


def normal_values(stream_key, shape, deviation, limit, cuts=(), held_as=jnp.bfloat16):
    values = deviation * jax.random.normal(stream_key, shape, jnp.float32)
    if cuts:
        values = values * shard_levels(stream_key, shape, cuts, -0.22, 0.18)
    return jnp.clip(values, -limit, limit).astype(held_as)


def setup_inputs(seed: int = 0) -> dict:
    key_list = jax.random.split(jax.random.key(seed), 15)
    layer_input = normal_values(key_list[0], (TOKENS, D), 1.0, 6.0, ((0, 16),))
    cotangent = normal_values(key_list[1], (TOKENS, D), 1.0, 6.0, ((0, 16),))
    segment_ids = draw_segment_ids(jax.random.fold_in(key_list[14], 71), 0)
    attend_weight = normal_values(key_list[3], (D, 3 * D), D ** -0.5, 0.21875, ((0, 16), (1, 2)), jnp.float32)
    output_weight = normal_values(key_list[4], (D, D), (D // 32) ** -0.5, 1.25, ((0, 16), (1, 2)), jnp.float32)
    widen_weight = normal_values(key_list[5], (D, FF), D ** -0.5, 0.21875, ((0, 16), (1, 2)), jnp.float32)
    narrow_weight = normal_values(key_list[6], (D, FF), FF ** -0.5, 0.109375, ((0, 16), (1, 2)), jnp.float32)
    attend_moment = draw_attend_moment(jax.random.fold_in(key_list[14], 71), 0)
    output_moment = draw_output_moment(jax.random.fold_in(key_list[14], 71), 0)
    widen_moment = draw_widen_moment(jax.random.fold_in(key_list[14], 71), 0)
    narrow_moment = draw_narrow_moment(jax.random.fold_in(key_list[14], 71), 0)
    vector_params = draw_vector_params(jax.random.fold_in(key_list[14], 71), 0)
    vector_first = draw_vector_first(jax.random.fold_in(key_list[14], 71), 0)
    vector_second = draw_vector_second(jax.random.fold_in(key_list[14], 71), 0)
    return dict(layer_input=layer_input, cotangent=cotangent, segment_ids=segment_ids, attend_weight=attend_weight, output_weight=output_weight, widen_weight=widen_weight, narrow_weight=narrow_weight, attend_moment=attend_moment, output_moment=output_moment, widen_moment=widen_moment, narrow_moment=narrow_moment, vector_params=vector_params, vector_first=vector_first, vector_second=vector_second)


@jax.custom_vjp
def low(v):
    return lax.optimization_barrier(v.astype(jnp.bfloat16)).astype(jnp.float32)

@jax.custom_vjp
def low_back(v):
    return v

def low_keep(v):
    return (low(v), None)

def low_pass(kept, grad):
    return (grad,)

def back_keep(v):
    return (v, None)

def back_low(kept, grad):
    return (low(grad),)
low.defvjp(low_keep, low_pass)
low_back.defvjp(back_keep, back_low)
HIGHEST = lax.Precision.HIGHEST
NORM_EPS = 1e-05
POLY_ONE = 3.4445
POLY_TWO = -4.775
POLY_THREE = 2.0315
SCALE_EPS = 1e-07
MUON_BETA = 0.9
MUON_RATE = 0.03
MUON_DECAY = 0.1
BETA_ONE = 0.9
BETA_TWO = 0.95
ADAM_RATE = 0.1
ADAM_EPS = 1e-08

def layer_norm(values, gain, shift):
    row_mean = lax.optimization_barrier(jnp.mean(values, axis=-1, keepdims=True))
    centered = values - row_mean
    row_var = lax.optimization_barrier(jnp.mean(centered * centered, axis=-1, keepdims=True))
    return centered * lax.rsqrt(row_var + NORM_EPS) * gain + shift

def rotate(values, cosines, sines):
    first_half = values[..., :ROTARY // 2]
    second_half = values[..., ROTARY // 2:ROTARY]
    remainder = values[..., ROTARY:]
    return jnp.concatenate([first_half * cosines - second_half * sines, second_half * cosines + first_half * sines, remainder], axis=-1)

def rotary_tables(segments):
    token_index = jnp.arange(segments.shape[0], dtype=jnp.int32)
    leading = jnp.sum((segments == 0).astype(jnp.int32))
    position = (token_index - jnp.where(segments == 1, leading, 0)).astype(jnp.float32)
    exponent = jnp.arange(ROTARY // 2, dtype=jnp.int32).astype(jnp.float32) * (2.0 / ROTARY)
    frequency = jnp.exp(-math.log(10000.0) * exponent)
    angles = position[:, None] * frequency[None, :]
    return (jnp.cos(angles)[:, None, :], jnp.sin(angles)[:, None, :])

def group_forward(group_input, segments, weights):
    attend_low, output_low, widen_low, narrow_low, vectors = weights
    length = group_input.shape[0]
    widen_rows = FF // D
    first_norm = low(layer_norm(group_input, vectors[0], vectors[1]))
    second_norm = low(layer_norm(group_input, vectors[2], vectors[3]))
    triple = low_back(jnp.dot(first_norm, attend_low, precision=HIGHEST) + vectors[4:7].reshape(-1))
    triple = triple.reshape(length, HEADS, 3, HEAD_DIM)
    cosines, sines = rotary_tables(segments)
    queries = low(low_back(rotate(triple[:, :, 0], cosines, sines)))
    key_heads = low(low_back(rotate(triple[:, :, 1], cosines, sines)))
    values = low(triple[:, :, 2])
    scores = low_back(jnp.einsum('qhd,khd->hqk', queries, key_heads, precision=HIGHEST) / math.sqrt(HEAD_DIM))
    token_index = jnp.arange(length, dtype=jnp.int32)
    allowed = (token_index[None, :] <= token_index[:, None]) & (segments[:, None] == segments[None, :])
    scores = jnp.where(allowed[None], scores, -jnp.inf)
    row_top = lax.optimization_barrier(jnp.max(scores, axis=-1, keepdims=True))
    exponent = jnp.exp(scores - row_top)
    softmax_low = low(exponent / lax.optimization_barrier(jnp.sum(exponent, axis=-1, keepdims=True)))
    mixture = jnp.einsum('hqk,khd->qhd', softmax_low, values, precision=HIGHEST).reshape(length, D)
    mixture = low(low_back(mixture))
    attended = jnp.dot(mixture, output_low.T, precision=HIGHEST)
    widened = low_back(jnp.dot(second_norm, widen_low, precision=HIGHEST) + vectors[8:8 + widen_rows].reshape(-1))
    activated = low(jax.nn.gelu(widened, approximate=False))
    narrowed = jnp.dot(activated, narrow_low.T, precision=HIGHEST)
    branch = low_back(attended + narrowed)
    live_rows = (segments >= 0).astype(jnp.float32)[:, None]
    return live_rows * (group_input + branch + vectors[7] + vectors[8 + widen_rows])

def forward(inputs, segment_ids, attend, output, widening, narrow, vectors):
    weights = (low(attend), low(output), low(widening), low(narrow), vectors)
    groups = inputs.shape[0] // DEV_TOK
    grouped = inputs.reshape(groups, DEV_TOK, D)
    segment_groups = segment_ids.reshape(groups, DEV_TOK)
    runner = jax.checkpoint(lambda members: group_forward(members[0], members[1], weights))
    return lax.map(runner, (grouped, segment_groups)).reshape(groups * DEV_TOK, D)

def orthogonal(matrix):
    norm_value = jnp.sqrt(jnp.sum(matrix * matrix))
    current = matrix / (norm_value + SCALE_EPS)
    for iteration in range(NS_STEPS):
        square = jnp.dot(current, current.T, precision=HIGHEST)
        polynomial = POLY_TWO * square + POLY_THREE * jnp.dot(square, square, precision=HIGHEST)
        current = POLY_ONE * current + jnp.dot(polynomial, current, precision=HIGHEST)
    return current

def reference(layer_input, cotangent, segment_ids, attend_weight, output_weight, widen_weight, narrow_weight, attend_moment, output_moment, widen_moment, narrow_moment, vector_params, vector_first, vector_second):

    def wrapped(inputs, attend, output, widening, narrow, vectors):
        return forward(inputs, segment_ids, attend, output, widening, narrow, vectors)
    result, pullback = jax.vjp(wrapped, layer_input.astype(jnp.float32), attend_weight, output_weight, widen_weight, narrow_weight, vector_params)
    gradients = pullback(cotangent.astype(jnp.float32))
    momenta = []
    updated = []
    for weight, moment, gradient in zip((attend_weight, output_weight, widen_weight, narrow_weight), (attend_moment, output_moment, widen_moment, narrow_moment), gradients[1:5]):
        momentum = MUON_BETA * moment + gradient
        orthogonal_part = orthogonal(momentum)
        step_scale = MUON_RATE * math.sqrt(max(weight.shape))
        momenta.append(momentum)
        updated.append(weight * (1.0 - MUON_RATE * MUON_DECAY) - step_scale * orthogonal_part)
    vector_grad = gradients[5]
    first_new = BETA_ONE * vector_first + (1.0 - BETA_ONE) * vector_grad
    second_new = BETA_TWO * vector_second + (1.0 - BETA_TWO) * vector_grad * vector_grad
    first_hat = first_new / (1.0 - BETA_ONE ** STEP)
    second_hat = second_new / (1.0 - BETA_TWO ** STEP)
    vectors_new = vector_params - ADAM_RATE * first_hat / (jnp.sqrt(second_hat) + ADAM_EPS)
    return (result.astype(jnp.bfloat16), gradients[0], gradients[1], gradients[2], gradients[3], gradients[4], momenta[0], momenta[1], momenta[2], momenta[3], updated[0], updated[1], updated[2], updated[3], vector_grad, first_new, second_new, vectors_new)
```

```python
import math

import jax
import jax.numpy as jnp
from jax import lax
from jax.sharding import PartitionSpec as P

D = 768
HEAD_DIM = 64
FF = 3072
ROTARY = 16
BLOCK = 512
NS_STEPS = 5
STEP = 10


HIGH = lax.Precision.HIGH
X_FIRST = (0, 1, 2)
Z_THEN_X = (2, 0, 1)
Z_THEN_Y = (2, 1, 0)
X_THEN_Y = (0, 1, 2)
Y_THEN_X = (1, 0, 2)
Z_FIRST = (2, 1, 0)
NORM_EPS = 1e-05
POLY_ONE = 3.4445
POLY_TWO = -4.775
POLY_THREE = 2.0315
SCALE_EPS = 1e-07
MUON_BETA = 0.9
MUON_RATE = 0.03
MUON_DECAY = 0.1
BETA_ONE = 0.9
BETA_TWO = 0.95
ADAM_RATE = 0.1
ADAM_EPS = 1e-08


DATA_AXES = {16: ((1, 2), (2, 2), (4, 4)), 128: ((1, 4), (4, 8), (32, 4))}


def data_axes(count):
    return DATA_AXES.get(count, ((1, count), (count, 1), (count, 1)))


def ring(count, stride, size):
    pairs = []
    for index in range(count):
        place = (index // stride) % size
        pairs.append((index, index + ((place + 1) % size - place) * stride))
    return pairs


def staged_gather(share, order):
    count = lax.axis_size("dp")
    rank = lax.axis_index("dp")
    rows, columns = share.shape
    held = share[None]
    sources = [rank]
    for axis in order:
        stride, size = data_axes(count)[axis]
        perm = ring(count, stride, size)
        parts, found = [held], list(sources)
        moving, owners = held, sources
        for _ in range(size - 1):
            moving = lax.ppermute(moving, "dp", perm)
            places = [(owner // stride) % size for owner in owners]
            owners = [
                owner + ((place + size - 1) % size - place) * stride
                for owner, place in zip(owners, places)
            ]
            parts.append(moving)
            found += owners
        held, sources = jnp.concatenate(parts, 0), found
    whole = jnp.zeros((count, rows, columns), share.dtype)
    for slot, source in enumerate(sources):
        whole = lax.dynamic_update_slice(whole, held[slot : slot + 1], (source, 0, 0))
    return whole.reshape(count * rows, columns)


def staged_scatter(partial, order):
    count = lax.axis_size("dp")
    rank = lax.axis_index("dp")
    axes = data_axes(count)
    rows, columns = partial.shape[0] // count, partial.shape[1]
    slow_first = sorted(range(len(axes)), key=lambda axis: -axes[axis][0])
    held = partial.reshape(*[axes[axis][1] for axis in slow_first], rows, columns)
    for axis in order:
        stride, size = axes[axis]
        if size == 1:
            continue
        perm = ring(count, stride, size)
        place = (rank // stride) % size
        dim = slow_first.index(axis)

        def block(target):
            return lax.dynamic_slice_in_dim(held, target % size, 1, dim)

        total = block(place + size - 1)
        for step in range(size - 1):
            got = lax.ppermute(total.astype(jnp.bfloat16), "dp", perm)
            total = block(place + 2 * size - 2 - step) + got.astype(jnp.float32)
        held = total
    return held.reshape(rows, columns)


def other_core(value):
    return lax.ppermute(value, "tensor", [(0, 1), (1, 0)])


def sum_everywhere(value):
    value = value + other_core(value)
    count = lax.axis_size("dp")
    distance = 1
    while distance < count:
        pairs = [(index, index ^ distance) for index in range(count)]
        value = value + lax.ppermute(value, "dp", pairs)
        distance *= 2
    return value


def product(left, right):
    return jnp.dot(left, right, precision=HIGH, preferred_element_type=jnp.float32)


def newton_rows(gram, first_row, rows):
    factor = 1.0 / (jnp.sqrt(jnp.trace(gram)) + SCALE_EPS)
    square = gram * (factor * factor)
    identity = jnp.eye(D, dtype=jnp.float32)
    kept = lax.dynamic_slice_in_dim(identity, first_row, rows, 0) * factor
    for iteration in range(NS_STEPS - 1):
        step = (
            POLY_ONE * identity + POLY_TWO * square + POLY_THREE * product(square, square)
        )
        kept = product(kept, step) if iteration else lax.dynamic_slice_in_dim(
            step, first_row, rows, 0
        ) * factor
        square = product(product(step, square), step)
    once = product(kept, square)
    return POLY_ONE * kept + POLY_TWO * once + POLY_THREE * product(once, square)


def rows_product(left, right):
    high = left.astype(jnp.bfloat16)
    low = (left - high.astype(jnp.float32)).astype(jnp.bfloat16)
    return jnp.dot(high, right, preferred_element_type=jnp.float32) + jnp.dot(
        low, right, preferred_element_type=jnp.float32
    )


def norm_stats(values):
    row_mean = jnp.mean(values, axis=-1, keepdims=True)
    centered = values - row_mean
    row_var = jnp.mean(centered * centered, axis=-1, keepdims=True)
    inverse = lax.rsqrt(row_var + NORM_EPS)
    return (centered * inverse, inverse)


def norm_backward(incoming, normed, inverse, gain):
    scaled = incoming * gain
    return inverse * (
        scaled
        - jnp.mean(scaled, axis=-1, keepdims=True)
        - normed * jnp.mean(scaled * normed, axis=-1, keepdims=True)
    )


def rotate(values, cosines, sines):
    first_half = values[..., : ROTARY // 2]
    second_half = values[..., ROTARY // 2 : ROTARY]
    remainder = values[..., ROTARY:]
    return jnp.concatenate(
        [
            first_half * cosines - second_half * sines,
            second_half * cosines + first_half * sines,
            remainder,
        ],
        axis=-1,
    )


def rotate_back(values, cosines, sines):
    first_half = values[..., : ROTARY // 2]
    second_half = values[..., ROTARY // 2 : ROTARY]
    remainder = values[..., ROTARY:]
    return jnp.concatenate(
        [
            first_half * cosines + second_half * sines,
            second_half * cosines - first_half * sines,
            remainder,
        ],
        axis=-1,
    )


def rotary_tables(segments):
    token_index = jnp.arange(segments.shape[0], dtype=jnp.int32)
    leading = jnp.sum((segments == 0).astype(jnp.int32))
    position = (token_index - jnp.where(segments == 1, leading, 0)).astype(jnp.float32)
    exponent = jnp.arange(ROTARY // 2, dtype=jnp.int32).astype(jnp.float32) * (2.0 / ROTARY)
    frequency = jnp.exp(-math.log(10000.0) * exponent)
    angles = position[:, None] * frequency[None, :]
    return (jnp.cos(angles)[:, None, :], jnp.sin(angles)[:, None, :])


def shards(
    layer_input,
    cotangent,
    segment_ids,
    attend_weight,
    output_weight,
    widen_weight,
    narrow_weight,
    attend_moment,
    output_moment,
    widen_moment,
    narrow_moment,
    vector_params,
    vector_first,
    vector_second,
):
    tensor_size = lax.axis_size("tensor")
    tensor_rank = lax.axis_index("tensor")
    data_size = lax.axis_size("dp")
    data_rank = lax.axis_index("dp")
    masters = (attend_weight, output_weight, widen_weight, narrow_weight)
    attend_columns = attend_weight.shape[1]
    widen_low = staged_gather(widen_weight.astype(jnp.bfloat16), Z_THEN_X)
    narrow_low = staged_gather(narrow_weight.astype(jnp.bfloat16), Z_THEN_Y)
    joint_low = staged_gather(
        jnp.concatenate([attend_weight, output_weight], 1).astype(jnp.bfloat16), X_FIRST
    )
    attend_low, output_low = joint_low[:, :attend_columns], joint_low[:, attend_columns:]
    length = layer_input.shape[0]
    triple_cols = attend_low.shape[1]
    local_heads = triple_cols // (3 * HEAD_DIM)
    widen_cols = widen_low.shape[1]
    widen_rows = FF // D
    feature_share = D // tensor_size
    blocks = length // BLOCK
    float_input = layer_input.astype(jnp.float32)
    first_gain = vector_params[0]
    second_gain = vector_params[2]
    attend_bias = lax.dynamic_slice_in_dim(
        vector_params[4:7].reshape(-1), tensor_rank * triple_cols, triple_cols
    )
    widen_bias = lax.dynamic_slice_in_dim(
        vector_params[8 : 8 + widen_rows].reshape(-1), tensor_rank * widen_cols, widen_cols
    )
    normed, inverse = norm_stats(float_input)
    first_norm = (normed * first_gain + vector_params[1]).astype(jnp.bfloat16)
    second_norm = (normed * second_gain + vector_params[3]).astype(jnp.bfloat16)
    triple = jnp.dot(first_norm, attend_low, preferred_element_type=jnp.float32) + attend_bias
    triple = triple.reshape(length, local_heads, 3, HEAD_DIM)
    cosines, sines = rotary_tables(segment_ids)
    queries = rotate(triple[:, :, 0], cosines, sines).astype(jnp.bfloat16)
    key_heads = rotate(triple[:, :, 1], cosines, sines).astype(jnp.bfloat16)
    values = triple[:, :, 2].astype(jnp.bfloat16)
    token_index = jnp.arange(length, dtype=jnp.int32)

    def block_scores(first_row):
        row_index = first_row + jnp.arange(BLOCK, dtype=jnp.int32)
        block_queries = lax.dynamic_slice_in_dim(queries, first_row, BLOCK, 0)
        block_segments = lax.dynamic_slice_in_dim(segment_ids, first_row, BLOCK, 0)
        scores = jnp.einsum(
            "qhd,khd->hqk", block_queries, key_heads, preferred_element_type=jnp.float32
        ) / math.sqrt(HEAD_DIM)
        allowed = (token_index[None, :] <= row_index[:, None]) & (
            segment_ids[None, :] == block_segments[:, None]
        )
        return jnp.where(allowed[None], scores, -jnp.inf)

    def attend_block(block_index):
        scores = block_scores(block_index * BLOCK)
        row_top = jnp.max(scores, axis=-1, keepdims=True)
        exponent = jnp.exp(scores - row_top)
        row_total = jnp.sum(exponent, axis=-1, keepdims=True)
        softmax_low = (exponent / row_total).astype(jnp.bfloat16)
        mixture = jnp.einsum(
            "hqk,khd->qhd", softmax_low, values, preferred_element_type=jnp.float32
        )
        return (mixture.astype(jnp.bfloat16), row_top + jnp.log(row_total))

    def attend_any(block_index):
        return attend_block(block_index)

    mixed_blocks, logsum = lax.map(attend_any, jnp.arange(blocks, dtype=jnp.int32))
    mixture = mixed_blocks.reshape(length, local_heads * HEAD_DIM)
    attended = jnp.einsum("sk,dk->sd", mixture, output_low, preferred_element_type=jnp.float32)
    widened = jnp.dot(second_norm, widen_low, preferred_element_type=jnp.float32) + widen_bias
    activated = jax.nn.gelu(widened, approximate=False).astype(jnp.bfloat16)
    narrowed = jnp.einsum("sf,df->sd", activated, narrow_low, preferred_element_type=jnp.float32)
    branch_part = attended + narrowed
    live_rows = (segment_ids >= 0).astype(jnp.float32)[:, None]
    column_start = tensor_rank * feature_share

    def own_columns(array):
        return lax.dynamic_slice_in_dim(array, column_start, feature_share, array.ndim - 1)

    other_start = (1 - tensor_rank) * feature_share
    branch = own_columns(branch_part) + other_core(
        lax.dynamic_slice_in_dim(branch_part, other_start, feature_share, 1)
    )
    block_output = (
        live_rows
        * (
            own_columns(float_input)
            + branch
            + own_columns(vector_params[7])
            + own_columns(vector_params[8 + widen_rows])
        )
    ).astype(jnp.bfloat16)
    upstream = live_rows * cotangent.astype(jnp.float32)
    upstream_low = upstream.astype(jnp.bfloat16)
    bias_grad = jnp.sum(upstream, axis=0) / tensor_size
    activation_grad = jnp.einsum(
        "sd,df->sf", upstream_low, narrow_low, preferred_element_type=jnp.float32
    )
    gelu_slope = jax.vjp(lambda inner_value: jax.nn.gelu(inner_value, approximate=False), widened)[
        1
    ](activation_grad)[0]
    widen_back = gelu_slope.astype(jnp.bfloat16)
    narrow_grad = jnp.einsum(
        "sd,sf->df", upstream_low, activated, preferred_element_type=jnp.float32
    )
    widen_grad = jnp.einsum(
        "sd,sf->df", second_norm, widen_back, preferred_element_type=jnp.float32
    )
    widen_bias_grad = jnp.sum(widen_back.astype(jnp.float32), axis=0)
    second_back = jnp.einsum("sf,df->sd", widen_back, widen_low, preferred_element_type=jnp.float32)
    mixed_grad = jnp.einsum(
        "sd,dk->sk", upstream_low, output_low, preferred_element_type=jnp.float32
    ).astype(jnp.bfloat16)
    output_grad = jnp.einsum("sd,sk->dk", upstream_low, mixture, preferred_element_type=jnp.float32)
    mixed_grad = mixed_grad.reshape(length, local_heads, HEAD_DIM)

    def backward_block(carried, block_index):
        key_grad, value_grad = carried
        first_row = block_index * BLOCK
        scores = block_scores(first_row)
        block_queries = lax.dynamic_slice_in_dim(queries, first_row, BLOCK, 0)
        block_mixed = lax.dynamic_slice_in_dim(mixed_grad, first_row, BLOCK, 0)
        softmax_rows = jnp.exp(scores - logsum[block_index])
        softmax_low = softmax_rows.astype(jnp.bfloat16)
        softmax_grad = jnp.einsum(
            "qhd,khd->hqk", block_mixed, values, preferred_element_type=jnp.float32
        )
        row_delta = jnp.sum(softmax_rows * softmax_grad, axis=-1, keepdims=True)
        score_grad = (softmax_rows * (softmax_grad - row_delta)).astype(jnp.bfloat16)
        query_grad = jnp.einsum(
            "hqk,khd->qhd", score_grad, key_heads, preferred_element_type=jnp.float32
        ) / math.sqrt(HEAD_DIM)
        key_grad = key_grad + jnp.einsum(
            "hqk,qhd->khd", score_grad, block_queries, preferred_element_type=jnp.float32
        ) / math.sqrt(HEAD_DIM)
        value_grad = value_grad + jnp.einsum(
            "hqk,qhd->khd", softmax_low, block_mixed, preferred_element_type=jnp.float32
        )
        return ((key_grad, value_grad), query_grad)

    def backward_any(carried, block_index):
        return backward_block(carried, block_index)

    zero_heads = jnp.zeros((length, local_heads, HEAD_DIM), jnp.float32)
    (key_grad, value_grad), query_blocks = lax.scan(
        backward_any, (zero_heads, zero_heads), jnp.arange(blocks, dtype=jnp.int32)
    )
    query_grad = query_blocks.reshape(length, local_heads, HEAD_DIM)
    query_back = rotate_back(
        lax.optimization_barrier(query_grad.astype(jnp.bfloat16)).astype(jnp.float32),
        cosines,
        sines,
    )
    key_back = rotate_back(
        lax.optimization_barrier(key_grad.astype(jnp.bfloat16)).astype(jnp.float32), cosines, sines
    )
    triple_grad = (
        jnp.stack([query_back, key_back, value_grad], axis=2)
        .reshape(length, triple_cols)
        .astype(jnp.bfloat16)
    )
    attend_grad = jnp.einsum(
        "sd,sk->dk", first_norm, triple_grad, preferred_element_type=jnp.float32
    )
    attend_bias_grad = jnp.sum(triple_grad.astype(jnp.float32), axis=0)
    first_back = jnp.einsum(
        "sk,dk->sd", triple_grad, attend_low, preferred_element_type=jnp.float32
    )
    row_share = length // tensor_size
    row_start = tensor_rank * row_share
    other_row = (1 - tensor_rank) * row_share

    def core_sum(part):
        sent = lax.dynamic_slice_in_dim(part, other_row, row_share, 0).astype(jnp.bfloat16)
        kept = lax.dynamic_slice_in_dim(part, row_start, row_share, 0)
        return kept + other_core(sent).astype(jnp.float32)

    first_total, second_total = core_sum(first_back), core_sum(second_back)
    normed_share = lax.dynamic_slice_in_dim(normed, row_start, row_share, 0)
    inverse_share = lax.dynamic_slice_in_dim(inverse, row_start, row_share, 0)
    upstream_share = lax.dynamic_slice_in_dim(upstream, row_start, row_share, 0)
    input_share = upstream_share + (
        norm_backward(first_total, normed_share, inverse_share, first_gain)
        + norm_backward(second_total, normed_share, inverse_share, second_gain)
    )
    input_low = input_share.astype(jnp.bfloat16)
    input_other = other_core(input_low)
    input_grad = jnp.where(
        tensor_rank == 0,
        jnp.concatenate([input_low, input_other], 0),
        jnp.concatenate([input_other, input_low], 0),
    ).astype(jnp.float32)
    norm_rows = jnp.stack(
        [
            jnp.sum(first_total * normed_share, axis=0),
            jnp.sum(first_total, axis=0),
            jnp.sum(second_total * normed_share, axis=0),
            jnp.sum(second_total, axis=0),
        ]
    )
    attend_bias_full = lax.dynamic_update_slice_in_dim(
        jnp.zeros((3 * D,), jnp.float32), attend_bias_grad, tensor_rank * triple_cols, 0
    )
    widen_bias_full = lax.dynamic_update_slice_in_dim(
        jnp.zeros((FF,), jnp.float32), widen_bias_grad, tensor_rank * widen_cols, 0
    )
    vector_part = jnp.concatenate(
        [
            norm_rows,
            attend_bias_full.reshape(3, D),
            bias_grad[None],
            widen_bias_full.reshape(widen_rows, D),
            bias_grad[None],
        ],
        axis=0,
    )
    vector_grad = sum_everywhere(vector_part)
    widen_sum = staged_scatter(widen_grad, X_THEN_Y)
    narrow_sum = staged_scatter(narrow_grad, Y_THEN_X)
    joint_sum = staged_scatter(jnp.concatenate([attend_grad, output_grad], 1), Z_FIRST)
    attend_sum, output_sum = joint_sum[:, :attend_columns], joint_sum[:, attend_columns:]
    summed = (attend_sum, output_sum, widen_sum, narrow_sum)
    moments = (attend_moment, output_moment, widen_moment, narrow_moment)
    momenta = [MUON_BETA * previous + gradient for previous, gradient in zip(moments, summed)]
    widths = [matrix.shape[1] for matrix in momenta]
    rows_here = D // data_size
    widen_whole = staged_gather(momenta[2].astype(jnp.bfloat16), Z_THEN_X)
    narrow_whole = staged_gather(momenta[3].astype(jnp.bfloat16), Z_THEN_Y)
    joint_whole = staged_gather(
        jnp.concatenate([momenta[0], momenta[1]], 1).astype(jnp.bfloat16), X_FIRST
    )
    wholes = [
        joint_whole[:, :attend_columns],
        joint_whole[:, attend_columns:],
        widen_whole,
        narrow_whole,
    ]

    def gram(matrix):
        return jnp.einsum("dk,ek->de", matrix, matrix, preferred_element_type=jnp.float32)

    def pair_rows(first, second):
        first_gram, second_gram = gram(first), gram(second)
        own = jnp.where(tensor_rank == 0, first_gram, second_gram)
        sent = jnp.where(tensor_rank == 0, second_gram, first_gram)
        rows = newton_rows(own + other_core(sent), data_rank * rows_here, rows_here)
        other = other_core(rows)
        return (
            jnp.where(tensor_rank == 0, rows, other),
            jnp.where(tensor_rank == 0, other, rows),
        )

    widen_rows_out, narrow_rows_out = pair_rows(wholes[2], wholes[3])
    attend_rows_out, output_rows_out = pair_rows(wholes[0], wholes[1])
    ortho_rows = (attend_rows_out, output_rows_out, widen_rows_out, narrow_rows_out)
    updated = []
    for matrix_index in range(4):
        longest = max(D, widths[matrix_index] * tensor_size)
        updated.append(
            masters[matrix_index] * (1.0 - MUON_RATE * MUON_DECAY)
            - MUON_RATE
            * math.sqrt(longest)
            * rows_product(ortho_rows[matrix_index], wholes[matrix_index])
        )
    first_new = BETA_ONE * vector_first + (1.0 - BETA_ONE) * vector_grad
    second_new = BETA_TWO * vector_second + (1.0 - BETA_TWO) * vector_grad * vector_grad
    first_hat = first_new / (1.0 - BETA_ONE**STEP)
    second_hat = second_new / (1.0 - BETA_TWO**STEP)
    vectors_new = vector_params - ADAM_RATE * first_hat / (jnp.sqrt(second_hat) + ADAM_EPS)
    return (
        block_output,
        input_grad,
        attend_sum,
        output_sum,
        widen_sum,
        narrow_sum,
        momenta[0],
        momenta[1],
        momenta[2],
        momenta[3],
        updated[0],
        updated[1],
        updated[2],
        updated[3],
        vector_grad,
        first_new,
        second_new,
        vectors_new,
    )


def solution(mesh):
    return jax.shard_map(
        shards,
        mesh=mesh,
        in_specs=(
            P("dp", None),
            P("dp", None),
            P("dp"),
            P("dp", "tensor"),
            P("dp", "tensor"),
            P("dp", "tensor"),
            P("dp", "tensor"),
            P("dp", "tensor"),
            P("dp", "tensor"),
            P("dp", "tensor"),
            P("dp", "tensor"),
            P(),
            P(),
            P(),
        ),
        out_specs=(
            P("dp", "tensor"),
            P("dp", None),
            P("dp", "tensor"),
            P("dp", "tensor"),
            P("dp", "tensor"),
            P("dp", "tensor"),
            P("dp", "tensor"),
            P("dp", "tensor"),
            P("dp", "tensor"),
            P("dp", "tensor"),
            P("dp", "tensor"),
            P("dp", "tensor"),
            P("dp", "tensor"),
            P("dp", "tensor"),
            P(),
            P(),
            P(),
            P(),
        ),
        check_vma=False,
    )
```

```python
import functools
import math

import jax
import jax.numpy as jnp
from jax import lax
from jax.experimental import pallas as pl
from jax.experimental.pallas import tpu as pltpu
from jax.sharding import PartitionSpec as P

D = 768
HEAD_DIM = 64
FF = 3072
ROTARY = 16
HALF = ROTARY // 2
NS_STEPS = 5
STEP = 10
QUERY_TILE = 512
VMEM_LIMIT = 48 * 1024 * 1024


HIGH = lax.Precision.HIGH
X_FIRST = (0, 1, 2)
Z_THEN_X = (2, 0, 1)
Z_THEN_Y = (2, 1, 0)
Z_ORDERS = (Z_THEN_X, Z_THEN_Y)
X_THEN_Y = (0, 1, 2)
Y_THEN_X = (1, 0, 2)
Z_FIRST = (2, 1, 0)
NORM_EPS = 1e-05
POLY_ONE = 3.4445
POLY_TWO = -4.775
POLY_THREE = 2.0315
SCALE_EPS = 1e-07
MUON_BETA = 0.9
MUON_RATE = 0.03
MUON_DECAY = 0.1
BETA_ONE = 0.9
BETA_TWO = 0.95
ADAM_RATE = 0.1
ADAM_EPS = 1e-08


DATA_AXES = {16: ((1, 2), (2, 2), (4, 4)), 128: ((1, 4), (4, 8), (32, 4))}


def data_axes(count):
    return DATA_AXES.get(count, ((1, count), (count, 1), (count, 1)))


def ring(count, stride, size):
    pairs = []
    for index in range(count):
        place = (index // stride) % size
        pairs.append((index, index + ((place + 1) % size - place) * stride))
    return pairs


def gather_sources(order, count, rank):
    sources = [rank]
    for axis in order:
        stride, size = data_axes(count)[axis]
        found, owners = list(sources), sources
        for _ in range(size - 1):
            places = [(owner // stride) % size for owner in owners]
            owners = [
                owner + ((place + size - 1) % size - place) * stride
                for owner, place in zip(owners, places)
            ]
            found += owners
        sources = found
    return sources


def place_kernel(orders, counts, width, count, *refs):
    parts, whole_ref, semaphores = list(refs[:-2]), refs[-2], refs[-1]
    copies = []
    for piece, order in enumerate(orders):
        sources = gather_sources(order, count, lax.axis_index("dp"))
        columns = pl.ds(piece * width, width)
        for part in [parts.pop(0) for _ in range(counts[piece])]:
            for row in range(part.shape[0]):
                copies.append(
                    pltpu.make_async_copy(
                        part.at[row],
                        whole_ref.at[sources.pop(0), :, columns],
                        semaphores.at[len(copies)],
                    )
                )
    for copy in copies:
        copy.start()
    for copy in copies:
        copy.wait()


def gather_stage(parts, axis):
    count = lax.axis_size("dp")
    stride, size = data_axes(count)[axis]
    perm = ring(count, stride, size)
    moving = jnp.concatenate(parts, 0) if len(parts) > 1 else parts[0]
    parts = [moving]
    for _ in range(size - 1):
        moving = lax.ppermute(moving, "dp", perm)
        parts.append(moving)
    return parts


def staged_gather(share, orders, early=(), late=()):
    count = lax.axis_size("dp")
    rows, columns = share.shape
    width = columns // len(orders)
    pieces = [
        [share[None, :, piece * width : (piece + 1) * width]] for piece in range(len(orders))
    ]
    for stage in range(3):
        pieces = [gather_stage(parts, order[stage]) for parts, order in zip(pieces, orders)]
        if stage == 0:
            pieces, early = lax.optimization_barrier((pieces, early))
    pieces, late = lax.optimization_barrier((pieces, late))
    anywhere = pl.BlockSpec(memory_space=pl.ANY)
    whole = pl.pallas_call(
        functools.partial(place_kernel, orders, [len(parts) for parts in pieces], width, count),
        in_specs=[anywhere] * sum(len(parts) for parts in pieces),
        out_specs=pl.BlockSpec(memory_space=pltpu.VMEM),
        out_shape=jax.ShapeDtypeStruct((count, rows, columns), share.dtype),
        scratch_shapes=[pltpu.SemaphoreType.DMA((count * len(orders),))],
        compiler_params=pltpu.CompilerParams(vmem_limit_bytes=VMEM_LIMIT),
        cost_estimate=pl.CostEstimate(
            flops=0, bytes_accessed=4 * count * rows * columns, transcendentals=0
        ),
    )(*[part for parts in pieces for part in parts])
    whole = whole.reshape(count * rows, columns)
    return whole, early, late


def staged_scatter(partial, order):
    count = lax.axis_size("dp")
    rank = lax.axis_index("dp")
    axes = data_axes(count)
    rows, columns = partial.shape[0] // count, partial.shape[1]
    slow_first = sorted(range(len(axes)), key=lambda axis: -axes[axis][0])
    held = partial.reshape(*[axes[axis][1] for axis in slow_first], rows, columns)
    for axis in order:
        stride, size = axes[axis]
        if size == 1:
            continue
        perm = ring(count, stride, size)
        place = (rank // stride) % size
        dim = slow_first.index(axis)

        def block(target):
            return lax.dynamic_slice_in_dim(held, target % size, 1, dim)

        total = block(place + size - 1)
        for step in range(size - 1):
            got = lax.ppermute(total.astype(jnp.bfloat16), "dp", perm)
            total = block(place + 2 * size - 2 - step) + got.astype(jnp.float32)
        held = total
    return held.reshape(rows, columns)


def other_core(value):
    return lax.ppermute(value, "tensor", [(0, 1), (1, 0)])


def sum_everywhere(value):
    value = value + other_core(value)
    count = lax.axis_size("dp")
    distance = 1
    while distance < count:
        pairs = [(index, index ^ distance) for index in range(count)]
        value = value + lax.ppermute(value, "dp", pairs)
        distance *= 2
    return value


def product(left, right):
    return jnp.dot(left, right, precision=HIGH, preferred_element_type=jnp.float32)


def newton_rows(gram, first_row, rows):
    factor = 1.0 / (jnp.sqrt(jnp.trace(gram)) + SCALE_EPS)
    square = gram * (factor * factor)
    identity = jnp.eye(D, dtype=jnp.float32)
    kept = lax.dynamic_slice_in_dim(identity, first_row, rows, 0) * factor
    for iteration in range(NS_STEPS - 1):
        step = (
            POLY_ONE * identity + POLY_TWO * square + POLY_THREE * product(square, square)
        )
        kept = product(kept, step) if iteration else lax.dynamic_slice_in_dim(
            step, first_row, rows, 0
        ) * factor
        square = product(product(step, square), step)
    once = product(kept, square)
    return POLY_ONE * kept + POLY_TWO * once + POLY_THREE * product(once, square)


def rows_product(left, right):
    high = left.astype(jnp.bfloat16)
    low = (left - high.astype(jnp.float32)).astype(jnp.bfloat16)
    return jnp.dot(high, right, preferred_element_type=jnp.float32) + jnp.dot(
        low, right, preferred_element_type=jnp.float32
    )


def norm_stats(values):
    row_mean = jnp.mean(values, axis=-1, keepdims=True)
    centered = values - row_mean
    row_var = jnp.mean(centered * centered, axis=-1, keepdims=True)
    inverse = lax.rsqrt(row_var + NORM_EPS)
    return (centered * inverse, inverse)


def norm_backward(incoming, normed, inverse, gain):
    scaled = incoming * gain
    return inverse * (
        scaled
        - jnp.mean(scaled, axis=-1, keepdims=True)
        - normed * jnp.mean(scaled * normed, axis=-1, keepdims=True)
    )


def rotary_tables(segments):
    token_index = jnp.arange(segments.shape[0], dtype=jnp.int32)
    leading = jnp.sum((segments == 0).astype(jnp.int32))
    position = (token_index - jnp.where(segments == 1, leading, 0)).astype(jnp.float32)
    exponent = jnp.arange(HALF, dtype=jnp.int32).astype(jnp.float32) * (2.0 / ROTARY)
    frequency = jnp.exp(-math.log(10000.0) * exponent)
    angles = frequency[:, None] * position[None, :]
    return (jnp.cos(angles), jnp.sin(angles))


def first_slots(segments):
    leading = jnp.sum((segments == 0).astype(jnp.int32))
    live = jnp.sum((segments >= 0).astype(jnp.int32))
    return jnp.where(segments == 0, 0, jnp.where(segments == 1, leading, live))


def matmul(left, right):
    return jnp.dot(left, right, preferred_element_type=jnp.float32)


def attention_kernel(
    triple_ref, cos_ref, sin_ref, upstream_ref, first_ref, mixture_ref, grad_ref, key_acc, value_acc
):
    length = triple_ref.shape[1]
    scale = 1.0 / math.sqrt(HEAD_DIM)
    cosines, sines = cos_ref[...], sin_ref[...]

    def turned(values, sign):
        first, second = values[:HALF], values[HALF:ROTARY]
        return jnp.concatenate(
            [
                first * cosines - sign * (second * sines),
                second * cosines + sign * (first * sines),
                values[ROTARY:],
            ],
            0,
        )

    def rounded(values):
        return values.astype(jnp.bfloat16).astype(jnp.float32)

    query_rows = rounded(turned(triple_ref[:HEAD_DIM], 1.0)) * scale
    key_rows = turned(triple_ref[HEAD_DIM : 2 * HEAD_DIM], 1.0)
    value_rows = triple_ref[2 * HEAD_DIM :]
    up_rows = upstream_ref[...]
    queries = query_rows.T.astype(jnp.bfloat16)
    keys = key_rows.T.astype(jnp.bfloat16)
    values = value_rows.T.astype(jnp.bfloat16)
    ups = up_rows.astype(jnp.float32).T.astype(jnp.bfloat16)
    query_rows = query_rows.astype(jnp.bfloat16)
    key_rows = key_rows.astype(jnp.bfloat16)
    value_rows = value_rows.astype(jnp.bfloat16)
    key_acc[...] = jnp.zeros_like(key_acc)
    value_acc[...] = jnp.zeros_like(value_acc)
    query_parts = []
    for tile in range(length // QUERY_TILE):
        start, stop = tile * QUERY_TILE, (tile + 1) * QUERY_TILE
        scores = matmul(keys[:stop], query_rows[:, start:stop])
        slot = lax.broadcasted_iota(jnp.int32, (stop, QUERY_TILE), 0)
        own = lax.broadcasted_iota(jnp.int32, (QUERY_TILE, QUERY_TILE), 1)
        keep = slot >= first_ref[:, start:stop]
        square = jnp.where(
            keep[start:] & (slot[:QUERY_TILE] <= own), scores[start:], -jnp.inf
        )
        if tile:
            scores = jnp.concatenate(
                [jnp.where(keep[:start], scores[:start], -jnp.inf), square], 0
            )
        else:
            scores = square
        top = jnp.max(scores, axis=0, keepdims=True)
        exponent = jnp.exp(scores - top)
        probs = exponent * (1.0 / jnp.sum(exponent, axis=0, keepdims=True))
        probs_low = probs.astype(jnp.bfloat16)
        mixture_ref[:, start:stop] = matmul(value_rows[:, :stop], probs_low).astype(jnp.bfloat16)
        prob_grad = matmul(values[:stop], up_rows[:, start:stop])
        delta = jnp.sum(probs * prob_grad, axis=0, keepdims=True)
        score_grad = (probs * (prob_grad - delta)).astype(jnp.bfloat16)
        query_parts.append(matmul(key_rows[:, :stop], score_grad))
        key_acc[:stop] += matmul(score_grad, queries[start:stop])
        value_acc[:stop] += matmul(probs_low, ups[start:stop])
    query_grad = rounded(jnp.concatenate(query_parts, 1) * scale)
    key_grad = rounded(key_acc[...].T)
    grad_ref[:HEAD_DIM] = turned(query_grad, -1.0).astype(jnp.bfloat16)
    grad_ref[HEAD_DIM : 2 * HEAD_DIM] = turned(key_grad, -1.0).astype(jnp.bfloat16)
    grad_ref[2 * HEAD_DIM :] = value_acc[...].T.astype(jnp.bfloat16)


def attention(triple_rows, cosines, sines, up_rows, segments):
    width, length = triple_rows.shape
    heads = width // (3 * HEAD_DIM)

    def whole(rows):
        return pl.BlockSpec((rows, length), lambda head: (0, 0))

    def own(rows):
        return pl.BlockSpec((rows, length), lambda head: (head, 0))

    return pl.pallas_call(
        attention_kernel,
        grid=(heads,),
        in_specs=[own(3 * HEAD_DIM), whole(HALF), whole(HALF), own(HEAD_DIM), whole(1)],
        out_specs=[own(HEAD_DIM), own(3 * HEAD_DIM)],
        out_shape=[
            jax.ShapeDtypeStruct((heads * HEAD_DIM, length), jnp.bfloat16),
            jax.ShapeDtypeStruct((width, length), jnp.bfloat16),
        ],
        scratch_shapes=[pltpu.VMEM((length, HEAD_DIM), jnp.float32)] * 2,
        compiler_params=pltpu.CompilerParams(vmem_limit_bytes=VMEM_LIMIT),
        cost_estimate=pl.CostEstimate(
            flops=heads * 36 * length * length * HEAD_DIM,
            bytes_accessed=width * length * 8,
            transcendentals=heads * length * length,
        ),
    )(triple_rows, cosines, sines, up_rows, first_slots(segments)[None])


def shards(
    layer_input,
    cotangent,
    segment_ids,
    attend_weight,
    output_weight,
    widen_weight,
    narrow_weight,
    attend_moment,
    output_moment,
    widen_moment,
    narrow_moment,
    vector_params,
    vector_first,
    vector_second,
):
    tensor_size = lax.axis_size("tensor")
    tensor_rank = lax.axis_index("tensor")
    data_size = lax.axis_size("dp")
    data_rank = lax.axis_index("dp")
    masters = (attend_weight, output_weight, widen_weight, narrow_weight)
    attend_columns = attend_weight.shape[1]
    attend_share = jnp.concatenate([attend_weight, output_weight], 1).astype(jnp.bfloat16)
    widen_low, narrow_share, _ = staged_gather(
        widen_weight.astype(jnp.bfloat16), Z_ORDERS, narrow_weight.astype(jnp.bfloat16)
    )
    length = layer_input.shape[0]
    triple_cols = attend_weight.shape[1]
    attend_columns = triple_cols
    widen_cols = widen_low.shape[1]
    widen_rows = FF // D
    feature_share = D // tensor_size
    float_input = layer_input.astype(jnp.float32)
    first_gain = vector_params[0]
    second_gain = vector_params[2]
    attend_bias = lax.dynamic_slice_in_dim(
        vector_params[4:7].reshape(-1), tensor_rank * triple_cols, triple_cols
    )
    widen_bias = lax.dynamic_slice_in_dim(
        vector_params[8 : 8 + widen_rows].reshape(-1), tensor_rank * widen_cols, widen_cols
    )
    normed, inverse = norm_stats(float_input)
    first_norm = (normed * first_gain + vector_params[1]).astype(jnp.bfloat16)
    second_norm = (normed * second_gain + vector_params[3]).astype(jnp.bfloat16)
    widened = jnp.dot(second_norm, widen_low, preferred_element_type=jnp.float32) + widen_bias
    activated = jax.nn.gelu(widened, approximate=False).astype(jnp.bfloat16)
    narrow_low, _, (widened, activated) = staged_gather(
        narrow_share, Z_ORDERS, late=(widened, activated)
    )
    live_rows = (segment_ids >= 0).astype(jnp.float32)[:, None]
    upstream = live_rows * cotangent.astype(jnp.float32)
    upstream_low = upstream.astype(jnp.bfloat16)
    bias_grad = jnp.sum(upstream, axis=0) / tensor_size
    activation_grad = jnp.einsum(
        "sd,df->sf", upstream_low, narrow_low, preferred_element_type=jnp.float32
    )
    gelu_slope = jax.vjp(lambda inner_value: jax.nn.gelu(inner_value, approximate=False), widened)[
        1
    ](activation_grad)[0]
    widen_back = gelu_slope.astype(jnp.bfloat16)
    narrow_grad = jnp.einsum(
        "sd,sf->df", upstream_low, activated, preferred_element_type=jnp.float32
    )
    widen_grad = jnp.einsum(
        "sd,sf->df", second_norm, widen_back, preferred_element_type=jnp.float32
    )
    widen_bias_grad = jnp.sum(widen_back.astype(jnp.float32), axis=0)
    second_back = jnp.einsum("sf,df->sd", widen_back, widen_low, preferred_element_type=jnp.float32)
    joint_low, _, (widen_grad, narrow_grad) = staged_gather(
        attend_share, (X_FIRST,), late=(widen_grad, narrow_grad)
    )
    attend_low, output_low = joint_low[:, :attend_columns], joint_low[:, attend_columns:]
    widen_sum = staged_scatter(widen_grad, X_THEN_Y)
    narrow_sum = staged_scatter(narrow_grad, Y_THEN_X)
    triple_rows = (
        jnp.einsum("dk,sd->ks", attend_low, first_norm, preferred_element_type=jnp.float32)
        + attend_bias[:, None]
    )
    mixed_rows = jnp.einsum(
        "sd,dk->ks", upstream_low, output_low, preferred_element_type=jnp.float32
    ).astype(jnp.bfloat16)
    cosines, sines = rotary_tables(segment_ids)
    mixture_rows, triple_grad = attention(triple_rows, cosines, sines, mixed_rows, segment_ids)
    output_grad = jnp.einsum(
        "sd,ks->dk", upstream_low, mixture_rows, preferred_element_type=jnp.float32
    )
    attend_grad = jnp.einsum(
        "sd,ks->dk", first_norm, triple_grad, preferred_element_type=jnp.float32
    )
    joint_sum = staged_scatter(jnp.concatenate([attend_grad, output_grad], 1), Z_FIRST)
    attend_bias_grad = jnp.sum(triple_grad.astype(jnp.float32), axis=1)
    first_back = jnp.einsum(
        "ks,dk->sd", triple_grad, attend_low, preferred_element_type=jnp.float32
    )
    attended = jnp.einsum(
        "ks,dk->sd", mixture_rows, output_low, preferred_element_type=jnp.float32
    )
    narrowed = jnp.einsum("sf,df->sd", activated, narrow_low, preferred_element_type=jnp.float32)
    branch_part = attended + narrowed
    column_start = tensor_rank * feature_share

    def own_columns(array):
        return lax.dynamic_slice_in_dim(array, column_start, feature_share, array.ndim - 1)

    other_start = (1 - tensor_rank) * feature_share
    branch = own_columns(branch_part) + other_core(
        lax.dynamic_slice_in_dim(branch_part, other_start, feature_share, 1)
    )
    block_output = (
        live_rows
        * (
            own_columns(float_input)
            + branch
            + own_columns(vector_params[7])
            + own_columns(vector_params[8 + widen_rows])
        )
    ).astype(jnp.bfloat16)
    row_share = length // tensor_size
    row_start = tensor_rank * row_share
    other_row = (1 - tensor_rank) * row_share

    def core_sum(part):
        sent = lax.dynamic_slice_in_dim(part, other_row, row_share, 0).astype(jnp.bfloat16)
        kept = lax.dynamic_slice_in_dim(part, row_start, row_share, 0)
        return kept + other_core(sent).astype(jnp.float32)

    first_total, second_total = core_sum(first_back), core_sum(second_back)
    normed_share = lax.dynamic_slice_in_dim(normed, row_start, row_share, 0)
    inverse_share = lax.dynamic_slice_in_dim(inverse, row_start, row_share, 0)
    upstream_share = lax.dynamic_slice_in_dim(upstream, row_start, row_share, 0)
    input_share = upstream_share + (
        norm_backward(first_total, normed_share, inverse_share, first_gain)
        + norm_backward(second_total, normed_share, inverse_share, second_gain)
    )
    input_low = input_share.astype(jnp.bfloat16)
    input_other = other_core(input_low)
    input_grad = jnp.where(
        tensor_rank == 0,
        jnp.concatenate([input_low, input_other], 0),
        jnp.concatenate([input_other, input_low], 0),
    ).astype(jnp.float32)
    norm_rows = jnp.stack(
        [
            jnp.sum(first_total * normed_share, axis=0),
            jnp.sum(first_total, axis=0),
            jnp.sum(second_total * normed_share, axis=0),
            jnp.sum(second_total, axis=0),
        ]
    )
    attend_bias_full = lax.dynamic_update_slice_in_dim(
        jnp.zeros((3 * D,), jnp.float32), attend_bias_grad, tensor_rank * triple_cols, 0
    )
    widen_bias_full = lax.dynamic_update_slice_in_dim(
        jnp.zeros((FF,), jnp.float32), widen_bias_grad, tensor_rank * widen_cols, 0
    )
    vector_part = jnp.concatenate(
        [
            norm_rows,
            attend_bias_full.reshape(3, D),
            bias_grad[None],
            widen_bias_full.reshape(widen_rows, D),
            bias_grad[None],
        ],
        axis=0,
    )
    vector_grad = sum_everywhere(vector_part)
    attend_sum, output_sum = joint_sum[:, :attend_columns], joint_sum[:, attend_columns:]
    summed = (attend_sum, output_sum, widen_sum, narrow_sum)
    moments = (attend_moment, output_moment, widen_moment, narrow_moment)
    momenta = [MUON_BETA * previous + gradient for previous, gradient in zip(moments, summed)]
    widths = [matrix.shape[1] for matrix in momenta]
    rows_here = D // data_size
    widen_whole, _, _ = staged_gather(momenta[2].astype(jnp.bfloat16), (Z_THEN_X,))
    narrow_whole, _, _ = staged_gather(momenta[3].astype(jnp.bfloat16), (Z_THEN_Y,))
    joint_moment = jnp.concatenate([momenta[0], momenta[1]], 1).astype(jnp.bfloat16)
    joint_moment, block_output, input_grad, vector_grad = lax.optimization_barrier(
        (joint_moment, block_output, input_grad, vector_grad)
    )
    joint_whole, _, _ = staged_gather(joint_moment, (X_FIRST,))
    wholes = [
        joint_whole[:, :attend_columns],
        joint_whole[:, attend_columns:],
        widen_whole,
        narrow_whole,
    ]

    def gram(matrix):
        return jnp.einsum("dk,ek->de", matrix, matrix, preferred_element_type=jnp.float32)

    parity = data_rank % 2
    even, low_core = parity == 0, tensor_rank == 0
    grams = [gram(matrix) for matrix in wholes]
    core_first = jnp.where(even, grams[2], grams[0])
    core_second = jnp.where(even, grams[3], grams[1])
    own_gram = jnp.where(low_core, core_first, core_second) + other_core(
        jnp.where(low_core, core_second, core_first)
    )
    pair_rows = newton_rows(own_gram, (data_rank - parity) * rows_here, 2 * rows_here)

    def rows_for(chip_parity):
        return lax.dynamic_slice_in_dim(pair_rows, chip_parity * rows_here, rows_here, 0)

    own_rows, near_rows = rows_for(parity), rows_for(1 - parity)
    devices = data_size * tensor_size

    def swapped(value, flip):
        pairs = [(index, index ^ flip) for index in range(devices)]
        return lax.ppermute(value, ("dp", "tensor"), pairs)

    core_rows, chip_rows, both_rows = (
        swapped(own_rows, 1),
        swapped(near_rows, tensor_size),
        swapped(near_rows, tensor_size + 1),
    )

    def pick(low, high):
        return jnp.where(low_core, low, high)

    here = (pick(own_rows, core_rows), pick(core_rows, own_rows))
    there = (pick(chip_rows, both_rows), pick(both_rows, chip_rows))
    ortho_rows = (
        jnp.where(even, there[0], here[0]),
        jnp.where(even, there[1], here[1]),
        jnp.where(even, here[0], there[0]),
        jnp.where(even, here[1], there[1]),
    )
    updated = []
    for matrix_index in range(4):
        longest = max(D, widths[matrix_index] * tensor_size)
        updated.append(
            masters[matrix_index] * (1.0 - MUON_RATE * MUON_DECAY)
            - MUON_RATE
            * math.sqrt(longest)
            * rows_product(ortho_rows[matrix_index], wholes[matrix_index])
        )
    first_new = BETA_ONE * vector_first + (1.0 - BETA_ONE) * vector_grad
    second_new = BETA_TWO * vector_second + (1.0 - BETA_TWO) * vector_grad * vector_grad
    first_hat = first_new / (1.0 - BETA_ONE**STEP)
    second_hat = second_new / (1.0 - BETA_TWO**STEP)
    vectors_new = vector_params - ADAM_RATE * first_hat / (jnp.sqrt(second_hat) + ADAM_EPS)
    return (
        block_output,
        input_grad,
        attend_sum,
        output_sum,
        widen_sum,
        narrow_sum,
        momenta[0],
        momenta[1],
        momenta[2],
        momenta[3],
        updated[0],
        updated[1],
        updated[2],
        updated[3],
        vector_grad,
        first_new,
        second_new,
        vectors_new,
    )


def solution(mesh):
    return jax.shard_map(
        shards,
        mesh=mesh,
        in_specs=(
            P("dp", None),
            P("dp", None),
            P("dp"),
            P("dp", "tensor"),
            P("dp", "tensor"),
            P("dp", "tensor"),
            P("dp", "tensor"),
            P("dp", "tensor"),
            P("dp", "tensor"),
            P("dp", "tensor"),
            P("dp", "tensor"),
            P(),
            P(),
            P(),
        ),
        out_specs=(
            P("dp", "tensor"),
            P("dp", None),
            P("dp", "tensor"),
            P("dp", "tensor"),
            P("dp", "tensor"),
            P("dp", "tensor"),
            P("dp", "tensor"),
            P("dp", "tensor"),
            P("dp", "tensor"),
            P("dp", "tensor"),
            P("dp", "tensor"),
            P("dp", "tensor"),
            P("dp", "tensor"),
            P("dp", "tensor"),
            P(),
            P(),
            P(),
            P(),
        ),
        check_vma=False,
    )
```

```python
import functools
import math

import jax
import jax.numpy as jnp
from jax import lax
from jax.experimental import pallas as pl
from jax.experimental.pallas import tpu as pltpu
from jax.sharding import PartitionSpec as P

D = 768
HEAD_DIM = 64
FF = 3072
ROTARY = 16
HALF = ROTARY // 2
NS_STEPS = 5
STEP = 10
QUERY_TILE = 512
VMEM_LIMIT = 48 * 1024 * 1024


HIGH = lax.Precision.HIGH
X_FIRST = (0, 1, 2)
Z_THEN_X = (2, 0, 1)
Z_THEN_Y = (2, 1, 0)
Z_ORDERS = (Z_THEN_X, Z_THEN_Y)
X_THEN_Y = (0, 1, 2)
Y_THEN_X = (1, 0, 2)
NORM_EPS = 1e-05
POLY_ONE = 3.4445
POLY_TWO = -4.775
POLY_THREE = 2.0315
SCALE_EPS = 1e-07
MUON_BETA = 0.9
MUON_RATE = 0.03
MUON_DECAY = 0.1
BETA_ONE = 0.9
BETA_TWO = 0.95
ADAM_RATE = 0.1
ADAM_EPS = 1e-08


DATA_AXES = {16: ((1, 2), (2, 2), (4, 4)), 128: ((1, 4), (4, 8), (32, 4))}


def data_axes(count):
    return DATA_AXES.get(count, ((1, count), (count, 1), (count, 1)))


def ring(count, stride, size):
    pairs = []
    for index in range(count):
        place = (index // stride) % size
        pairs.append((index, index + ((place + 1) % size - place) * stride))
    return pairs


def gather_sources(order, count, rank):
    sources = [rank]
    for axis in order:
        stride, size = data_axes(count)[axis]
        found, owners = list(sources), sources
        for _ in range(size - 1):
            places = [(owner // stride) % size for owner in owners]
            owners = [
                owner + ((place + size - 1) % size - place) * stride
                for owner, place in zip(owners, places)
            ]
            found += owners
        sources = found
    return sources


def place_kernel(orders, counts, width, count, *refs):
    parts, whole_ref, semaphores = list(refs[:-2]), refs[-2], refs[-1]
    copies = []
    for piece, order in enumerate(orders):
        sources = gather_sources(order, count, lax.axis_index("dp"))
        columns = pl.ds(piece * width, width)
        for part in [parts.pop(0) for _ in range(counts[piece])]:
            for row in range(part.shape[0]):
                copies.append(
                    pltpu.make_async_copy(
                        part.at[row],
                        whole_ref.at[sources.pop(0), :, columns],
                        semaphores.at[len(copies)],
                    )
                )
    for copy in copies:
        copy.start()
    for copy in copies:
        copy.wait()


def gather_steps(share, orders):
    count = lax.axis_size("dp")
    width = share.shape[1] // len(orders)
    pieces = [
        [share[None, :, piece * width : (piece + 1) * width]] for piece in range(len(orders))
    ]
    hops = sum(size - 1 for _, size in data_axes(count))
    plans = [
        [(axis, hop) for axis in order for hop in range(data_axes(count)[axis][1] - 1)]
        for order in orders
    ]
    moving = [None] * len(orders)
    for step in range(hops):
        for piece, plan in enumerate(plans):
            axis, hop = plan[step]
            stride, size = data_axes(count)[axis]
            if hop == 0:
                parts = pieces[piece]
                moving[piece] = jnp.concatenate(parts, 0) if len(parts) > 1 else parts[0]
                pieces[piece] = [moving[piece]]
            moving[piece] = lax.ppermute(moving[piece], "dp", ring(count, stride, size))
        moving = list((yield moving))
        for parts, part in zip(pieces, moving):
            parts.append(part)
    return pieces


def scatter_steps(partial, order):
    count = lax.axis_size("dp")
    rank = lax.axis_index("dp")
    axes = data_axes(count)
    rows, columns = partial.shape[0] // count, partial.shape[1]
    slow_first = sorted(range(len(axes)), key=lambda axis: -axes[axis][0])
    held = partial.reshape(*[axes[axis][1] for axis in slow_first], rows, columns)
    for axis in order:
        stride, size = axes[axis]
        if size == 1:
            continue
        perm = ring(count, stride, size)
        place = (rank // stride) % size
        dim = slow_first.index(axis)

        def block(target):
            return lax.dynamic_slice_in_dim(held, target % size, 1, dim)

        total = block(place + size - 1)
        for step in range(size - 1):
            (got,) = yield [lax.ppermute(total.astype(jnp.bfloat16), "dp", perm)]
            total = block(place + 2 * size - 2 - step) + got.astype(jnp.float32)
        held = total
    return held.reshape(rows, columns)


class Travel:
    def __init__(self, steps):
        self.steps = steps
        self.moving = None
        self.result = None

    def hop(self):
        if self.result is None:
            try:
                self.moving = self.steps.send(self.moving)
            except StopIteration as stop:
                self.moving = []
                self.result = stop.value

    def finish(self):
        while self.result is None:
            self.hop()
        return self.result


def hop_all(*travels):
    for travel in travels:
        travel.hop()


def arrived(travels, beside):
    moving, beside = lax.optimization_barrier(([travel.moving for travel in travels], beside))
    for travel, value in zip(travels, moving):
        travel.moving = value
    return beside


def placed(pieces, orders):
    count = lax.axis_size("dp")
    rows, width = pieces[0][0].shape[1:]
    dtype = pieces[0][0].dtype
    anywhere = pl.BlockSpec(memory_space=pl.ANY)
    whole = pl.pallas_call(
        functools.partial(place_kernel, orders, [len(parts) for parts in pieces], width, count),
        in_specs=[anywhere] * sum(len(parts) for parts in pieces),
        out_specs=pl.BlockSpec(memory_space=pltpu.VMEM),
        out_shape=jax.ShapeDtypeStruct((count, rows, width * len(orders)), dtype),
        scratch_shapes=[pltpu.SemaphoreType.DMA((count * len(orders),))],
        compiler_params=pltpu.CompilerParams(vmem_limit_bytes=VMEM_LIMIT),
        cost_estimate=pl.CostEstimate(
            flops=0, bytes_accessed=4 * count * rows * width * len(orders), transcendentals=0
        ),
    )(*[part for parts in pieces for part in parts])
    return whole.reshape(count * rows, width * len(orders))


def other_core(value):
    return lax.ppermute(value, "tensor", [(0, 1), (1, 0)])


def sum_steps(value):
    (got,) = yield [other_core(value)]
    value = value + got
    count = lax.axis_size("dp")
    distance = 1
    while distance < count:
        pairs = [(index, index ^ distance) for index in range(count)]
        (got,) = yield [lax.ppermute(value, "dp", pairs)]
        value = value + got
        distance *= 2
    return value


def product(left, right):
    return jnp.dot(left, right, precision=HIGH, preferred_element_type=jnp.float32)


def newton_rows(gram, first_row, rows):
    factor = 1.0 / (jnp.sqrt(jnp.trace(gram)) + SCALE_EPS)
    square = gram * (factor * factor)
    identity = jnp.eye(D, dtype=jnp.float32)
    kept = lax.dynamic_slice_in_dim(identity, first_row, rows, 0) * factor
    for iteration in range(NS_STEPS - 1):
        step = (
            POLY_ONE * identity + POLY_TWO * square + POLY_THREE * product(square, square)
        )
        kept = product(kept, step) if iteration else lax.dynamic_slice_in_dim(
            step, first_row, rows, 0
        ) * factor
        square = product(product(step, square), step)
    once = product(kept, square)
    return POLY_ONE * kept + POLY_TWO * once + POLY_THREE * product(once, square)


def rows_product(left, right):
    high = left.astype(jnp.bfloat16)
    low = (left - high.astype(jnp.float32)).astype(jnp.bfloat16)
    return jnp.dot(high, right, preferred_element_type=jnp.float32) + jnp.dot(
        low, right, preferred_element_type=jnp.float32
    )


def norm_stats(values):
    row_mean = jnp.mean(values, axis=-1, keepdims=True)
    centered = values - row_mean
    row_var = jnp.mean(centered * centered, axis=-1, keepdims=True)
    inverse = lax.rsqrt(row_var + NORM_EPS)
    return (centered * inverse, inverse)


def norm_backward(incoming, normed, inverse, gain):
    scaled = incoming * gain
    return inverse * (
        scaled
        - jnp.mean(scaled, axis=-1, keepdims=True)
        - normed * jnp.mean(scaled * normed, axis=-1, keepdims=True)
    )


def rotary_tables(segments):
    token_index = jnp.arange(segments.shape[0], dtype=jnp.int32)
    leading = jnp.sum((segments == 0).astype(jnp.int32))
    position = (token_index - jnp.where(segments == 1, leading, 0)).astype(jnp.float32)
    exponent = jnp.arange(HALF, dtype=jnp.int32).astype(jnp.float32) * (2.0 / ROTARY)
    frequency = jnp.exp(-math.log(10000.0) * exponent)
    angles = frequency[:, None] * position[None, :]
    return (jnp.cos(angles), jnp.sin(angles))


def first_slots(segments):
    leading = jnp.sum((segments == 0).astype(jnp.int32))
    live = jnp.sum((segments >= 0).astype(jnp.int32))
    return jnp.where(segments == 0, 0, jnp.where(segments == 1, leading, live))


def matmul(left, right):
    return jnp.dot(left, right, preferred_element_type=jnp.float32)


def attention_kernel(
    triple_ref, cos_ref, sin_ref, upstream_ref, first_ref, mixture_ref, grad_ref, key_acc, value_acc
):
    length = triple_ref.shape[1]
    scale = 1.0 / math.sqrt(HEAD_DIM)
    cosines, sines = cos_ref[...], sin_ref[...]

    def turned(values, sign):
        first, second = values[:HALF], values[HALF:ROTARY]
        return jnp.concatenate(
            [
                first * cosines - sign * (second * sines),
                second * cosines + sign * (first * sines),
                values[ROTARY:],
            ],
            0,
        )

    def rounded(values):
        return values.astype(jnp.bfloat16).astype(jnp.float32)

    query_rows = rounded(turned(triple_ref[:HEAD_DIM], 1.0)) * scale
    key_rows = turned(triple_ref[HEAD_DIM : 2 * HEAD_DIM], 1.0)
    value_rows = triple_ref[2 * HEAD_DIM :]
    up_rows = upstream_ref[...]
    queries = query_rows.T.astype(jnp.bfloat16)
    keys = key_rows.T.astype(jnp.bfloat16)
    values = value_rows.T.astype(jnp.bfloat16)
    ups = up_rows.astype(jnp.float32).T.astype(jnp.bfloat16)
    query_rows = query_rows.astype(jnp.bfloat16)
    key_rows = key_rows.astype(jnp.bfloat16)
    value_rows = value_rows.astype(jnp.bfloat16)
    key_acc[...] = jnp.zeros_like(key_acc)
    value_acc[...] = jnp.zeros_like(value_acc)
    query_parts = []
    for tile in range(length // QUERY_TILE):
        start, stop = tile * QUERY_TILE, (tile + 1) * QUERY_TILE
        scores = matmul(keys[:stop], query_rows[:, start:stop])
        slot = lax.broadcasted_iota(jnp.int32, (stop, QUERY_TILE), 0)
        own = lax.broadcasted_iota(jnp.int32, (QUERY_TILE, QUERY_TILE), 1)
        keep = slot >= first_ref[:, start:stop]
        square = jnp.where(
            keep[start:] & (slot[:QUERY_TILE] <= own), scores[start:], -jnp.inf
        )
        if tile:
            scores = jnp.concatenate(
                [jnp.where(keep[:start], scores[:start], -jnp.inf), square], 0
            )
        else:
            scores = square
        top = jnp.max(scores, axis=0, keepdims=True)
        exponent = jnp.exp(scores - top)
        probs = exponent * (1.0 / jnp.sum(exponent, axis=0, keepdims=True))
        probs_low = probs.astype(jnp.bfloat16)
        mixture_ref[:, start:stop] = matmul(value_rows[:, :stop], probs_low).astype(jnp.bfloat16)
        prob_grad = matmul(values[:stop], up_rows[:, start:stop])
        delta = jnp.sum(probs * prob_grad, axis=0, keepdims=True)
        score_grad = (probs * (prob_grad - delta)).astype(jnp.bfloat16)
        query_parts.append(matmul(key_rows[:, :stop], score_grad))
        key_acc[:stop] += matmul(score_grad, queries[start:stop])
        value_acc[:stop] += matmul(probs_low, ups[start:stop])
    query_grad = rounded(jnp.concatenate(query_parts, 1) * scale)
    key_grad = rounded(key_acc[...].T)
    grad_ref[:HEAD_DIM] = turned(query_grad, -1.0).astype(jnp.bfloat16)
    grad_ref[HEAD_DIM : 2 * HEAD_DIM] = turned(key_grad, -1.0).astype(jnp.bfloat16)
    grad_ref[2 * HEAD_DIM :] = value_acc[...].T.astype(jnp.bfloat16)


def attention(triple_rows, cosines, sines, up_rows, segments):
    width, length = triple_rows.shape
    heads = width // (3 * HEAD_DIM)

    def whole(rows):
        return pl.BlockSpec((rows, length), lambda head: (0, 0))

    def own(rows):
        return pl.BlockSpec((rows, length), lambda head: (head, 0))

    return pl.pallas_call(
        attention_kernel,
        grid=(heads,),
        in_specs=[own(3 * HEAD_DIM), whole(HALF), whole(HALF), own(HEAD_DIM), whole(1)],
        out_specs=[own(HEAD_DIM), own(3 * HEAD_DIM)],
        out_shape=[
            jax.ShapeDtypeStruct((heads * HEAD_DIM, length), jnp.bfloat16),
            jax.ShapeDtypeStruct((width, length), jnp.bfloat16),
        ],
        scratch_shapes=[pltpu.VMEM((length, HEAD_DIM), jnp.float32)] * 2,
        compiler_params=pltpu.CompilerParams(vmem_limit_bytes=VMEM_LIMIT),
        cost_estimate=pl.CostEstimate(
            flops=heads * 36 * length * length * HEAD_DIM,
            bytes_accessed=width * length * 8,
            transcendentals=heads * length * length,
        ),
    )(triple_rows, cosines, sines, up_rows, first_slots(segments)[None])


def shards(
    layer_input,
    cotangent,
    segment_ids,
    attend_weight,
    output_weight,
    widen_weight,
    narrow_weight,
    attend_moment,
    output_moment,
    widen_moment,
    narrow_moment,
    vector_params,
    vector_first,
    vector_second,
):
    tensor_size = lax.axis_size("tensor")
    tensor_rank = lax.axis_index("tensor")
    data_size = lax.axis_size("dp")
    data_rank = lax.axis_index("dp")
    masters = (attend_weight, output_weight, widen_weight, narrow_weight)
    length = layer_input.shape[0]
    triple_cols = attend_weight.shape[1]
    widen_cols = widen_weight.shape[1]
    widen_rows = FF // D
    feature_share = D // tensor_size
    widen_order, narrow_order = (Z_THEN_X,), (Z_THEN_Y,)

    joint_gather = Travel(
        gather_steps(
            jnp.concatenate([attend_weight, output_weight], 1).astype(jnp.bfloat16), Z_ORDERS
        )
    )
    joint_gather.hop()
    widen_share, narrow_share = arrived(
        [joint_gather], (widen_weight.astype(jnp.bfloat16), narrow_weight.astype(jnp.bfloat16))
    )
    widen_gather = Travel(gather_steps(widen_share, widen_order))
    narrow_gather = Travel(gather_steps(narrow_share, narrow_order))
    feeds = (widen_gather, narrow_gather)
    joint_gather.hop()
    layer_input, cotangent = arrived([joint_gather], (layer_input, cotangent))
    joint_gather.hop()
    float_input = layer_input.astype(jnp.float32)
    first_gain = vector_params[0]
    second_gain = vector_params[2]
    attend_bias = lax.dynamic_slice_in_dim(
        vector_params[4:7].reshape(-1), tensor_rank * triple_cols, triple_cols
    )
    widen_bias = lax.dynamic_slice_in_dim(
        vector_params[8 : 8 + widen_rows].reshape(-1), tensor_rank * widen_cols, widen_cols
    )
    normed, inverse = norm_stats(float_input)
    inverse = arrived([joint_gather], inverse)
    hop_all(joint_gather, *feeds)
    first_norm = (normed * first_gain + vector_params[1]).astype(jnp.bfloat16)
    second_norm = (normed * second_gain + vector_params[3]).astype(jnp.bfloat16)
    first_norm, second_norm = arrived([joint_gather, *feeds], (first_norm, second_norm))
    hop_all(joint_gather, *feeds)
    hop_all(*feeds)
    live_rows = (segment_ids >= 0).astype(jnp.float32)[:, None]
    upstream = live_rows * cotangent.astype(jnp.float32)
    upstream_low = upstream.astype(jnp.bfloat16)
    bias_grad = jnp.sum(upstream, axis=0) / tensor_size
    cosines, sines = rotary_tables(segment_ids)
    upstream_low, bias_grad, cosines, sines = arrived(
        [joint_gather, *feeds], (upstream_low, bias_grad, cosines, sines)
    )
    hop_all(*feeds)
    joint_low = placed(joint_gather.finish(), Z_ORDERS)
    attend_low, output_low = joint_low[:, :triple_cols], joint_low[:, triple_cols:]
    triple_rows = (
        jnp.einsum("dk,sd->ks", attend_low, first_norm, preferred_element_type=jnp.float32)
        + attend_bias[:, None]
    )
    mixed_rows = jnp.einsum(
        "sd,dk->ks", upstream_low, output_low, preferred_element_type=jnp.float32
    ).astype(jnp.bfloat16)
    triple_rows, mixed_rows = arrived(feeds, (triple_rows, mixed_rows))
    hop_all(*feeds)
    mixture_rows, triple_grad = attention(triple_rows, cosines, sines, mixed_rows, segment_ids)
    mixture_rows, triple_grad = arrived(feeds, (mixture_rows, triple_grad))
    output_grad = jnp.einsum(
        "sd,ks->dk", upstream_low, mixture_rows, preferred_element_type=jnp.float32
    )
    attend_grad = jnp.einsum(
        "sd,ks->dk", first_norm, triple_grad, preferred_element_type=jnp.float32
    )
    joint_scatter = Travel(
        scatter_steps(jnp.concatenate([attend_grad, output_grad], 1), X_THEN_Y)
    )
    widen_low = placed(widen_gather.finish(), widen_order)
    narrow_low = placed(narrow_gather.finish(), narrow_order)

    joint_scatter.hop()
    widened = jnp.dot(second_norm, widen_low, preferred_element_type=jnp.float32) + widen_bias
    activated = jax.nn.gelu(widened, approximate=False).astype(jnp.bfloat16)
    widened, activated = arrived([joint_scatter], (widened, activated))
    joint_scatter.hop()
    activation_grad = jnp.einsum(
        "sd,df->sf", upstream_low, narrow_low, preferred_element_type=jnp.float32
    )
    gelu_slope = jax.vjp(lambda inner_value: jax.nn.gelu(inner_value, approximate=False), widened)[
        1
    ](activation_grad)[0]
    widen_back = gelu_slope.astype(jnp.bfloat16)
    narrow_grad = jnp.einsum(
        "sd,sf->df", upstream_low, activated, preferred_element_type=jnp.float32
    )
    widen_grad = jnp.einsum(
        "sd,sf->df", second_norm, widen_back, preferred_element_type=jnp.float32
    )
    widen_grad, narrow_grad, widen_back = arrived(
        [joint_scatter], (widen_grad, narrow_grad, widen_back)
    )
    widen_scatter = Travel(scatter_steps(widen_grad, X_THEN_Y))
    narrow_scatter = Travel(scatter_steps(narrow_grad, Y_THEN_X))
    sums = (widen_scatter, narrow_scatter)
    hop_all(*sums, joint_scatter)
    hop_all(joint_scatter)
    hop_all(joint_scatter)
    row_share = length // tensor_size
    row_start = tensor_rank * row_share
    other_row = (1 - tensor_rank) * row_share

    def core_sum(part):
        sent = lax.dynamic_slice_in_dim(part, other_row, row_share, 0).astype(jnp.bfloat16)
        kept = lax.dynamic_slice_in_dim(part, row_start, row_share, 0)
        return kept + other_core(sent).astype(jnp.float32)

    second_back = jnp.einsum("sf,df->sd", widen_back, widen_low, preferred_element_type=jnp.float32)
    first_back = jnp.einsum(
        "ks,dk->sd", triple_grad, attend_low, preferred_element_type=jnp.float32
    )
    first_total, second_total = core_sum(first_back), core_sum(second_back)
    attended = jnp.einsum(
        "ks,dk->sd", mixture_rows, output_low, preferred_element_type=jnp.float32
    )
    narrowed = jnp.einsum("sf,df->sd", activated, narrow_low, preferred_element_type=jnp.float32)
    branch_part = attended + narrowed
    column_start = tensor_rank * feature_share

    def own_columns(array):
        return lax.dynamic_slice_in_dim(array, column_start, feature_share, array.ndim - 1)

    other_start = (1 - tensor_rank) * feature_share
    branch = own_columns(branch_part) + other_core(
        lax.dynamic_slice_in_dim(branch_part, other_start, feature_share, 1)
    )
    block_output = (
        live_rows
        * (
            own_columns(float_input)
            + branch
            + own_columns(vector_params[7])
            + own_columns(vector_params[8 + widen_rows])
        )
    ).astype(jnp.bfloat16)
    widen_bias_grad = jnp.sum(widen_back.astype(jnp.float32), axis=0)
    attend_bias_grad = jnp.sum(triple_grad.astype(jnp.float32), axis=1)
    first_total, second_total, block_output, widen_bias_grad, attend_bias_grad = arrived(
        [*sums, joint_scatter],
        (first_total, second_total, block_output, widen_bias_grad, attend_bias_grad),
    )
    joint_sum = joint_scatter.finish()
    attend_sum, output_sum = joint_sum[:, :triple_cols], joint_sum[:, triple_cols:]
    attend_momentum = MUON_BETA * attend_moment + attend_sum
    output_momentum = MUON_BETA * output_moment + output_sum
    joint_gather = Travel(
        gather_steps(
            jnp.concatenate([attend_momentum, output_momentum], 1).astype(jnp.bfloat16), Z_ORDERS
        )
    )
    hop_all(*sums, joint_gather)
    hop_all(joint_gather)
    normed_share = lax.dynamic_slice_in_dim(normed, row_start, row_share, 0)
    inverse_share = lax.dynamic_slice_in_dim(inverse, row_start, row_share, 0)
    upstream_share = lax.dynamic_slice_in_dim(upstream, row_start, row_share, 0)
    input_share = upstream_share + (
        norm_backward(first_total, normed_share, inverse_share, first_gain)
        + norm_backward(second_total, normed_share, inverse_share, second_gain)
    )
    input_low = input_share.astype(jnp.bfloat16)
    input_other = other_core(input_low)
    input_grad = jnp.where(
        tensor_rank == 0,
        jnp.concatenate([input_low, input_other], 0),
        jnp.concatenate([input_other, input_low], 0),
    ).astype(jnp.float32)
    norm_rows = jnp.stack(
        [
            jnp.sum(first_total * normed_share, axis=0),
            jnp.sum(first_total, axis=0),
            jnp.sum(second_total * normed_share, axis=0),
            jnp.sum(second_total, axis=0),
        ]
    )
    attend_bias_full = lax.dynamic_update_slice_in_dim(
        jnp.zeros((3 * D,), jnp.float32), attend_bias_grad, tensor_rank * triple_cols, 0
    )
    widen_bias_full = lax.dynamic_update_slice_in_dim(
        jnp.zeros((FF,), jnp.float32), widen_bias_grad, tensor_rank * widen_cols, 0
    )
    vector_part = jnp.concatenate(
        [
            norm_rows,
            attend_bias_full.reshape(3, D),
            bias_grad[None],
            widen_bias_full.reshape(widen_rows, D),
            bias_grad[None],
        ],
        axis=0,
    )
    input_grad, vector_part = arrived([*sums, joint_gather], (input_grad, vector_part))
    vector_sum = Travel(sum_steps(vector_part))
    for _ in range(3):
        hop_all(*sums, joint_gather, vector_sum)
        arrived([*sums, joint_gather, vector_sum], ())
    widen_sum, narrow_sum = widen_scatter.finish(), narrow_scatter.finish()
    widen_momentum = MUON_BETA * widen_moment + widen_sum
    narrow_momentum = MUON_BETA * narrow_moment + narrow_sum
    widen_gather = Travel(gather_steps(widen_momentum.astype(jnp.bfloat16), widen_order))
    narrow_gather = Travel(gather_steps(narrow_momentum.astype(jnp.bfloat16), narrow_order))
    feeds = (widen_gather, narrow_gather)
    hop_all(*feeds, vector_sum)

    def gram(matrix):
        return jnp.einsum("dk,ek->de", matrix, matrix, preferred_element_type=jnp.float32)

    joint_whole = placed(joint_gather.finish(), Z_ORDERS)
    attend_whole, output_whole = joint_whole[:, :triple_cols], joint_whole[:, triple_cols:]
    attend_gram, output_gram = gram(attend_whole), gram(output_whole)
    attend_gram, output_gram = arrived([*feeds, vector_sum], (attend_gram, output_gram))
    hop_all(*feeds, vector_sum)
    arrived([*feeds, vector_sum], ())
    hop_all(*feeds)
    vector_grad = arrived(feeds, vector_sum.finish())
    hop_all(*feeds)
    arrived(feeds, ())
    hop_all(*feeds)
    widen_whole = placed(widen_gather.finish(), widen_order)
    narrow_whole = placed(narrow_gather.finish(), narrow_order)
    grams = (attend_gram, output_gram, gram(widen_whole), gram(narrow_whole))
    summed = (attend_sum, output_sum, widen_sum, narrow_sum)
    momenta = (attend_momentum, output_momentum, widen_momentum, narrow_momentum)
    widths = [matrix.shape[1] for matrix in momenta]
    rows_here = D // data_size
    wholes = (attend_whole, output_whole, widen_whole, narrow_whole)
    parity = data_rank % 2
    even, low_core = parity == 0, tensor_rank == 0
    core_first = jnp.where(even, grams[2], grams[0])
    core_second = jnp.where(even, grams[3], grams[1])
    own_gram = jnp.where(low_core, core_first, core_second) + other_core(
        jnp.where(low_core, core_second, core_first)
    )
    pair_rows = newton_rows(own_gram, (data_rank - parity) * rows_here, 2 * rows_here)

    def rows_for(chip_parity):
        return lax.dynamic_slice_in_dim(pair_rows, chip_parity * rows_here, rows_here, 0)

    own_rows, near_rows = rows_for(parity), rows_for(1 - parity)
    devices = data_size * tensor_size

    def swapped(value, flip):
        pairs = [(index, index ^ flip) for index in range(devices)]
        return lax.ppermute(value, ("dp", "tensor"), pairs)

    core_rows, chip_rows, both_rows = (
        swapped(own_rows, 1),
        swapped(near_rows, tensor_size),
        swapped(near_rows, tensor_size + 1),
    )

    def pick(low, high):
        return jnp.where(low_core, low, high)

    here = (pick(own_rows, core_rows), pick(core_rows, own_rows))
    there = (pick(chip_rows, both_rows), pick(both_rows, chip_rows))
    ortho_rows = (
        jnp.where(even, there[0], here[0]),
        jnp.where(even, there[1], here[1]),
        jnp.where(even, here[0], there[0]),
        jnp.where(even, here[1], there[1]),
    )
    updated = []
    for matrix_index in range(4):
        longest = max(D, widths[matrix_index] * tensor_size)
        updated.append(
            masters[matrix_index] * (1.0 - MUON_RATE * MUON_DECAY)
            - MUON_RATE
            * math.sqrt(longest)
            * rows_product(ortho_rows[matrix_index], wholes[matrix_index])
        )
    first_new = BETA_ONE * vector_first + (1.0 - BETA_ONE) * vector_grad
    second_new = BETA_TWO * vector_second + (1.0 - BETA_TWO) * vector_grad * vector_grad
    first_hat = first_new / (1.0 - BETA_ONE**STEP)
    second_hat = second_new / (1.0 - BETA_TWO**STEP)
    vectors_new = vector_params - ADAM_RATE * first_hat / (jnp.sqrt(second_hat) + ADAM_EPS)
    return (
        block_output,
        input_grad,
        attend_sum,
        output_sum,
        widen_sum,
        narrow_sum,
        momenta[0],
        momenta[1],
        momenta[2],
        momenta[3],
        updated[0],
        updated[1],
        updated[2],
        updated[3],
        vector_grad,
        first_new,
        second_new,
        vectors_new,
    )


def solution(mesh):
    return jax.shard_map(
        shards,
        mesh=mesh,
        in_specs=(
            P("dp", None),
            P("dp", None),
            P("dp"),
            P("dp", "tensor"),
            P("dp", "tensor"),
            P("dp", "tensor"),
            P("dp", "tensor"),
            P("dp", "tensor"),
            P("dp", "tensor"),
            P("dp", "tensor"),
            P("dp", "tensor"),
            P(),
            P(),
            P(),
        ),
        out_specs=(
            P("dp", "tensor"),
            P("dp", None),
            P("dp", "tensor"),
            P("dp", "tensor"),
            P("dp", "tensor"),
            P("dp", "tensor"),
            P("dp", "tensor"),
            P("dp", "tensor"),
            P("dp", "tensor"),
            P("dp", "tensor"),
            P("dp", "tensor"),
            P("dp", "tensor"),
            P("dp", "tensor"),
            P("dp", "tensor"),
            P(),
            P(),
            P(),
            P(),
        ),
        check_vma=False,
    )
```

```python
import functools
import math

import jax
import jax.numpy as jnp
from jax import lax
from jax.experimental import pallas as pl
from jax.experimental.pallas import tpu as pltpu
from jax.sharding import PartitionSpec as P

D = 768
HEAD_DIM = 64
FF = 3072
ROTARY = 16
HALF = ROTARY // 2
NS_STEPS = 5
STEP = 10
QUERY_TILE = 512
FEED_TILE = 512
NEWTON_TILE = 256
VMEM_LIMIT = 48 * 1024 * 1024


X_FIRST = (0, 1, 2)
Z_THEN_X = (2, 0, 1)
Z_THEN_Y = (2, 1, 0)
Z_ORDERS = (Z_THEN_X, Z_THEN_Y)
X_THEN_Y = (0, 1, 2)
Y_THEN_X = (1, 0, 2)
NORM_EPS = 1e-05
POLY_ONE = 3.4445
POLY_TWO = -4.775
POLY_THREE = 2.0315
SCALE_EPS = 1e-07
MUON_BETA = 0.9
MUON_RATE = 0.03
MUON_DECAY = 0.1
BETA_ONE = 0.9
BETA_TWO = 0.95
ADAM_RATE = 0.1
ADAM_EPS = 1e-08


DATA_AXES = {16: ((1, 2), (2, 2), (4, 4)), 128: ((1, 4), (4, 8), (32, 4))}


def data_axes(count):
    return DATA_AXES.get(count, ((1, count), (count, 1), (count, 1)))


def ring(count, stride, size):
    pairs = []
    for index in range(count):
        place = (index // stride) % size
        pairs.append((index, index + ((place + 1) % size - place) * stride))
    return pairs


def gather_sources(order, count, rank):
    sources = [rank]
    for axis in order:
        stride, size = data_axes(count)[axis]
        found, owners = list(sources), sources
        for _ in range(size - 1):
            places = [(owner // stride) % size for owner in owners]
            owners = [
                owner + ((place + size - 1) % size - place) * stride
                for owner, place in zip(owners, places)
            ]
            found += owners
        sources = found
    return sources


def place_kernel(orders, counts, width, count, *refs):
    parts, whole_ref, semaphores = list(refs[:-2]), refs[-2], refs[-1]
    copies = []
    for piece, order in enumerate(orders):
        sources = gather_sources(order, count, lax.axis_index("dp"))
        columns = pl.ds(piece * width, width)
        for part in [parts.pop(0) for _ in range(counts[piece])]:
            for row in range(part.shape[0]):
                copies.append(
                    pltpu.make_async_copy(
                        part.at[row],
                        whole_ref.at[sources.pop(0), :, columns],
                        semaphores.at[len(copies)],
                    )
                )
    for copy in copies:
        copy.start()
    for copy in copies:
        copy.wait()


def gather_steps(share, orders):
    count = lax.axis_size("dp")
    width = share.shape[1] // len(orders)
    pieces = [
        [share[None, :, piece * width : (piece + 1) * width]] for piece in range(len(orders))
    ]
    hops = sum(size - 1 for _, size in data_axes(count))
    plans = [
        [(axis, hop) for axis in order for hop in range(data_axes(count)[axis][1] - 1)]
        for order in orders
    ]
    moving = [None] * len(orders)
    for step in range(hops):
        for piece, plan in enumerate(plans):
            axis, hop = plan[step]
            stride, size = data_axes(count)[axis]
            if hop == 0:
                parts = pieces[piece]
                moving[piece] = jnp.concatenate(parts, 0) if len(parts) > 1 else parts[0]
                pieces[piece] = [moving[piece]]
            moving[piece] = lax.ppermute(moving[piece], "dp", ring(count, stride, size))
        moving = list((yield moving))
        for parts, part in zip(pieces, moving):
            parts.append(part)
    return pieces


def scatter_steps(partial, order):
    count = lax.axis_size("dp")
    rank = lax.axis_index("dp")
    axes = data_axes(count)
    rows, columns = partial.shape[0] // count, partial.shape[1]
    slow_first = sorted(range(len(axes)), key=lambda axis: -axes[axis][0])
    held = partial.reshape(*[axes[axis][1] for axis in slow_first], rows, columns)
    for axis in order:
        stride, size = axes[axis]
        if size == 1:
            continue
        perm = ring(count, stride, size)
        place = (rank // stride) % size
        dim = slow_first.index(axis)

        def block(target):
            return lax.dynamic_slice_in_dim(held, target % size, 1, dim)

        total = block(place + size - 1)
        for step in range(size - 1):
            (got,) = yield [lax.ppermute(total.astype(jnp.bfloat16), "dp", perm)]
            total = block(place + 2 * size - 2 - step) + got.astype(jnp.float32)
        held = total
    return held.reshape(rows, columns)


class Travel:
    def __init__(self, steps):
        self.steps = steps
        self.moving = None
        self.result = None

    def hop(self):
        if self.result is None:
            try:
                self.moving = self.steps.send(self.moving)
            except StopIteration as stop:
                self.moving = []
                self.result = stop.value

    def finish(self):
        while self.result is None:
            self.hop()
        return self.result


def hop_all(*travels):
    for travel in travels:
        travel.hop()


def arrived(travels, beside):
    moving, beside = lax.optimization_barrier(([travel.moving for travel in travels], beside))
    for travel, value in zip(travels, moving):
        travel.moving = value
    return beside


def placed(pieces, orders):
    count = lax.axis_size("dp")
    rows, width = pieces[0][0].shape[1:]
    dtype = pieces[0][0].dtype
    anywhere = pl.BlockSpec(memory_space=pl.ANY)
    whole = pl.pallas_call(
        functools.partial(place_kernel, orders, [len(parts) for parts in pieces], width, count),
        in_specs=[anywhere] * sum(len(parts) for parts in pieces),
        out_specs=pl.BlockSpec(memory_space=pltpu.VMEM),
        out_shape=jax.ShapeDtypeStruct((count, rows, width * len(orders)), dtype),
        scratch_shapes=[pltpu.SemaphoreType.DMA((count * len(orders),))],
        compiler_params=pltpu.CompilerParams(vmem_limit_bytes=VMEM_LIMIT),
        cost_estimate=pl.CostEstimate(
            flops=0, bytes_accessed=4 * count * rows * width * len(orders), transcendentals=0
        ),
    )(*[part for parts in pieces for part in parts])
    return whole.reshape(count * rows, width * len(orders))


def other_core(value):
    return lax.ppermute(value, "tensor", [(0, 1), (1, 0)])


def sum_steps(value):
    (got,) = yield [other_core(value)]
    value = value + got
    count = lax.axis_size("dp")
    distance = 1
    while distance < count:
        pairs = [(index, index ^ distance) for index in range(count)]
        (got,) = yield [lax.ppermute(value, "dp", pairs)]
        value = value + got
        distance *= 2
    return value


def rows_product(left, right):
    high = left.astype(jnp.bfloat16)
    low = (left - high.astype(jnp.float32)).astype(jnp.bfloat16)
    return jnp.dot(high, right, preferred_element_type=jnp.float32) + jnp.dot(
        low, right, preferred_element_type=jnp.float32
    )


def norm_stats(values):
    row_mean = jnp.mean(values, axis=-1, keepdims=True)
    centered = values - row_mean
    row_var = jnp.mean(centered * centered, axis=-1, keepdims=True)
    inverse = lax.rsqrt(row_var + NORM_EPS)
    return (centered * inverse, inverse)


def norm_backward(incoming, normed, inverse, gain):
    scaled = incoming * gain
    return inverse * (
        scaled
        - jnp.mean(scaled, axis=-1, keepdims=True)
        - normed * jnp.mean(scaled * normed, axis=-1, keepdims=True)
    )


def rotary_tables(segments):
    token_index = jnp.arange(segments.shape[0], dtype=jnp.int32)
    leading = jnp.sum((segments == 0).astype(jnp.int32))
    position = (token_index - jnp.where(segments == 1, leading, 0)).astype(jnp.float32)
    exponent = jnp.arange(HALF, dtype=jnp.int32).astype(jnp.float32) * (2.0 / ROTARY)
    frequency = jnp.exp(-math.log(10000.0) * exponent)
    angles = frequency[:, None] * position[None, :]
    return (jnp.cos(angles), jnp.sin(angles))


def first_slots(segments):
    leading = jnp.sum((segments == 0).astype(jnp.int32))
    live = jnp.sum((segments >= 0).astype(jnp.int32))
    return jnp.where(segments == 0, 0, jnp.where(segments == 1, leading, live))


def matmul(left, right):
    return jnp.dot(left, right, preferred_element_type=jnp.float32)


def attention_kernel(
    triple_ref, cos_ref, sin_ref, upstream_ref, first_ref, mixture_ref, grad_ref, key_acc, value_acc
):
    length = triple_ref.shape[1]
    scale = 1.0 / math.sqrt(HEAD_DIM)
    cosines, sines = cos_ref[...], sin_ref[...]

    def turned(values, sign):
        first, second = values[:HALF], values[HALF:ROTARY]
        return jnp.concatenate(
            [
                first * cosines - sign * (second * sines),
                second * cosines + sign * (first * sines),
                values[ROTARY:],
            ],
            0,
        )

    def rounded(values):
        return values.astype(jnp.bfloat16).astype(jnp.float32)

    query_rows = rounded(turned(triple_ref[:HEAD_DIM], 1.0)) * scale
    key_rows = turned(triple_ref[HEAD_DIM : 2 * HEAD_DIM], 1.0)
    value_rows = triple_ref[2 * HEAD_DIM :]
    up_rows = upstream_ref[...]
    queries = query_rows.T.astype(jnp.bfloat16)
    keys = key_rows.T.astype(jnp.bfloat16)
    values = value_rows.T.astype(jnp.bfloat16)
    ups = up_rows.astype(jnp.float32).T.astype(jnp.bfloat16)
    query_rows = query_rows.astype(jnp.bfloat16)
    key_rows = key_rows.astype(jnp.bfloat16)
    value_rows = value_rows.astype(jnp.bfloat16)
    key_acc[...] = jnp.zeros_like(key_acc)
    value_acc[...] = jnp.zeros_like(value_acc)
    query_parts = []
    for tile in range(length // QUERY_TILE):
        start, stop = tile * QUERY_TILE, (tile + 1) * QUERY_TILE
        scores = matmul(keys[:stop], query_rows[:, start:stop])
        slot = lax.broadcasted_iota(jnp.int32, (stop, QUERY_TILE), 0)
        own = lax.broadcasted_iota(jnp.int32, (QUERY_TILE, QUERY_TILE), 1)
        keep = slot >= first_ref[:, start:stop]
        square = jnp.where(
            keep[start:] & (slot[:QUERY_TILE] <= own), scores[start:], -jnp.inf
        )
        if tile:
            scores = jnp.concatenate(
                [jnp.where(keep[:start], scores[:start], -jnp.inf), square], 0
            )
        else:
            scores = square
        top = jnp.max(scores, axis=0, keepdims=True)
        exponent = jnp.exp(scores - top)
        probs = exponent * (1.0 / jnp.sum(exponent, axis=0, keepdims=True))
        probs_low = probs.astype(jnp.bfloat16)
        mixture_ref[:, start:stop] = matmul(value_rows[:, :stop], probs_low).astype(jnp.bfloat16)
        prob_grad = matmul(values[:stop], up_rows[:, start:stop])
        delta = jnp.sum(probs * prob_grad, axis=0, keepdims=True)
        score_grad = (probs * (prob_grad - delta)).astype(jnp.bfloat16)
        query_parts.append(matmul(key_rows[:, :stop], score_grad))
        key_acc[:stop] += matmul(score_grad, queries[start:stop])
        value_acc[:stop] += matmul(probs_low, ups[start:stop])
    query_grad = rounded(jnp.concatenate(query_parts, 1) * scale)
    key_grad = rounded(key_acc[...].T)
    grad_ref[:HEAD_DIM] = turned(query_grad, -1.0).astype(jnp.bfloat16)
    grad_ref[HEAD_DIM : 2 * HEAD_DIM] = turned(key_grad, -1.0).astype(jnp.bfloat16)
    grad_ref[2 * HEAD_DIM :] = value_acc[...].T.astype(jnp.bfloat16)


def attention(triple_rows, cosines, sines, up_rows, segments):
    width, length = triple_rows.shape
    heads = width // (3 * HEAD_DIM)

    def whole(rows):
        return pl.BlockSpec((rows, length), lambda head: (0, 0))

    def own(rows):
        return pl.BlockSpec((rows, length), lambda head: (head, 0))

    return pl.pallas_call(
        attention_kernel,
        grid=(heads,),
        in_specs=[own(3 * HEAD_DIM), whole(HALF), whole(HALF), own(HEAD_DIM), whole(1)],
        out_specs=[own(HEAD_DIM), own(3 * HEAD_DIM)],
        out_shape=[
            jax.ShapeDtypeStruct((heads * HEAD_DIM, length), jnp.bfloat16),
            jax.ShapeDtypeStruct((width, length), jnp.bfloat16),
        ],
        scratch_shapes=[pltpu.VMEM((length, HEAD_DIM), jnp.float32)] * 2,
        compiler_params=pltpu.CompilerParams(vmem_limit_bytes=VMEM_LIMIT),
        cost_estimate=pl.CostEstimate(
            flops=heads * 36 * length * length * HEAD_DIM,
            bytes_accessed=width * length * 8,
            transcendentals=heads * length * length,
        ),
    )(triple_rows, cosines, sines, up_rows, first_slots(segments)[None])


def split(value):
    high = value.astype(jnp.bfloat16)
    return high, (value - high.astype(jnp.float32)).astype(jnp.bfloat16)


def newton_kernel(first_ref, second_ref, rows_ref, out_ref, square, square_parts, step, left):
    wanted = rows_ref.shape[0]
    tiles = D // NEWTON_TILE

    def store_split(ref, rows, columns, value):
        high, low = split(value)
        ref[0, rows, columns] = high
        ref[1, rows, columns] = low

    def product(left_ref, rows, right_ref, columns):
        left_high, left_low = left_ref[0, rows, :], left_ref[1, rows, :]
        right_high, right_low = right_ref[0, :, columns], right_ref[1, :, columns]
        return matmul(left_high, right_high) + (
            matmul(left_high, right_low) + matmul(left_low, right_high)
        )

    def part(tile):
        return slice(tile * NEWTON_TILE, (tile + 1) * NEWTON_TILE)

    def both(store, row, column, value):
        store(part(row), part(column), value)
        if row != column:
            store(part(column), part(row), value.T)

    def put(rows, columns, value):
        square[rows, columns] = value
        store_split(square_parts, rows, columns, value)

    def diagonal(size):
        return lax.broadcasted_iota(jnp.int32, (size, size), 0) == lax.broadcasted_iota(
            jnp.int32, (size, size), 1
        )

    whole, extra = slice(None), slice(D, D + wanted)
    gram = first_ref[...] + second_ref[...]
    trace = jnp.sum(jnp.where(diagonal(D), gram, 0.0), axis=0, keepdims=True)
    trace = jnp.sum(trace, axis=1, keepdims=True)
    factor = 1.0 / (jnp.sqrt(trace) + SCALE_EPS)
    put(whole, whole, gram * (factor * factor))
    rows_value = rows_ref[...] * factor
    store_split(left, extra, whole, rows_value)
    identity = jnp.where(diagonal(NEWTON_TILE), POLY_ONE, 0.0)
    for _ in range(NS_STEPS - 1):
        for column in range(tiles):
            top = slice(0, (column + 1) * NEWTON_TILE)
            value = POLY_TWO * square[top, part(column)] + POLY_THREE * product(
                square_parts, top, square_parts, part(column)
            )
            for row in range(column + 1):
                block = value[part(row)]
                if row == column:
                    block = block + identity
                both(functools.partial(store_split, step), row, column, block)
        for column in range(tiles):
            top = slice(0, (column + 1) * NEWTON_TILE)
            value = product(step, top, square_parts, part(column))
            for row in range(column + 1):
                both(functools.partial(store_split, left), row, column, value[part(row)])
        rows_parts = []
        for column in range(tiles):
            top = slice(0, (column + 1) * NEWTON_TILE)
            value = product(left, top, step, part(column))
            rows_parts.append(product(left, extra, step, part(column)))
            for row in range(column + 1):
                both(put, row, column, value[part(row)])
        rows_value = jnp.concatenate(rows_parts, 1)
        store_split(left, extra, whole, rows_value)

    def by_square():
        return jnp.concatenate(
            [product(left, extra, square_parts, part(column)) for column in range(tiles)], 1
        )

    once = by_square()
    store_split(left, extra, whole, once)
    out_ref[...] = POLY_ONE * rows_value + POLY_TWO * once + POLY_THREE * by_square()


def newton_rows(own_gram, other_gram, first_row, rows):
    wanted = -(-rows // 16) * 16
    index = lax.broadcasted_iota(jnp.int32, (wanted, D), 0)
    chosen = lax.broadcasted_iota(jnp.int32, (wanted, D), 1) == index + first_row
    rows_out = pl.pallas_call(
        newton_kernel,
        in_specs=[pl.BlockSpec(memory_space=pltpu.VMEM)] * 3,
        out_specs=pl.BlockSpec(memory_space=pltpu.VMEM),
        out_shape=jax.ShapeDtypeStruct((wanted, D), jnp.float32),
        scratch_shapes=[
            pltpu.VMEM((D, D), jnp.float32),
            pltpu.VMEM((2, D, D), jnp.bfloat16),
            pltpu.VMEM((2, D, D), jnp.bfloat16),
            pltpu.VMEM((2, D + wanted, D), jnp.bfloat16),
        ],
        compiler_params=pltpu.CompilerParams(vmem_limit_bytes=VMEM_LIMIT),
        cost_estimate=pl.CostEstimate(
            flops=(NS_STEPS - 1) * 12 * D * D * D, bytes_accessed=8 * D * D, transcendentals=0
        ),
    )(own_gram, other_gram, chosen.astype(jnp.float32))
    return rows_out[:rows]


def feed_kernel(
    norm_ref, upstream_ref, widen_ref, narrow_ref, bias_ref, activated_ref, back_ref, sum_ref
):
    widened = matmul(norm_ref[...], widen_ref[...]) + bias_ref[...]
    incoming = matmul(upstream_ref[...], narrow_ref[...])
    area = 0.5 + 0.5 * lax.erf(widened * math.sqrt(0.5))
    density = jnp.exp(widened * widened * -0.5) * (1.0 / math.sqrt(2.0 * math.pi))
    activated_ref[...] = (widened * area).astype(jnp.bfloat16)
    back = (incoming * (area + widened * density)).astype(jnp.bfloat16)
    back_ref[...] = back
    sum_ref[...] = jnp.sum(back.astype(jnp.float32), axis=0, keepdims=True)


def feed_forward(norm, upstream, widen, narrow, bias):
    length, width = norm.shape
    hidden = widen.shape[1]

    def whole():
        return pl.BlockSpec((length, width), lambda tile: (0, 0))

    def columns(rows):
        return pl.BlockSpec((rows, FEED_TILE), lambda tile: (0, tile))

    return pl.pallas_call(
        feed_kernel,
        grid=(hidden // FEED_TILE,),
        in_specs=[whole(), whole(), columns(width), columns(width), columns(1)],
        out_specs=[columns(length), columns(length), columns(1)],
        out_shape=[jax.ShapeDtypeStruct((length, hidden), jnp.bfloat16)] * 2
        + [jax.ShapeDtypeStruct((1, hidden), jnp.float32)],
        compiler_params=pltpu.CompilerParams(vmem_limit_bytes=VMEM_LIMIT),
        cost_estimate=pl.CostEstimate(
            flops=4 * length * width * hidden,
            bytes_accessed=4 * length * (width + hidden) + 4 * width * hidden,
            transcendentals=4 * length * hidden,
        ),
    )(norm, upstream, widen, narrow, bias[None])


def shards(
    layer_input,
    cotangent,
    segment_ids,
    attend_weight,
    output_weight,
    widen_weight,
    narrow_weight,
    attend_moment,
    output_moment,
    widen_moment,
    narrow_moment,
    vector_params,
    vector_first,
    vector_second,
):
    tensor_size = lax.axis_size("tensor")
    tensor_rank = lax.axis_index("tensor")
    data_size = lax.axis_size("dp")
    data_rank = lax.axis_index("dp")
    masters = (attend_weight, output_weight, widen_weight, narrow_weight)
    length = layer_input.shape[0]
    triple_cols = attend_weight.shape[1]
    widen_cols = widen_weight.shape[1]
    widen_rows = FF // D
    feature_share = D // tensor_size
    widen_order, narrow_order = (Z_THEN_X,), (Z_THEN_Y,)

    joint_gather = Travel(
        gather_steps(
            jnp.concatenate([attend_weight, output_weight], 1).astype(jnp.bfloat16), Z_ORDERS
        )
    )
    joint_gather.hop()
    widen_share, narrow_share = arrived(
        [joint_gather], (widen_weight.astype(jnp.bfloat16), narrow_weight.astype(jnp.bfloat16))
    )
    widen_gather = Travel(gather_steps(widen_share, widen_order))
    narrow_gather = Travel(gather_steps(narrow_share, narrow_order))
    feeds = (widen_gather, narrow_gather)
    joint_gather.hop()
    layer_input, cotangent = arrived([joint_gather], (layer_input, cotangent))
    joint_gather.hop()
    float_input = layer_input.astype(jnp.float32)
    first_gain = vector_params[0]
    second_gain = vector_params[2]
    attend_bias = lax.dynamic_slice_in_dim(
        vector_params[4:7].reshape(-1), tensor_rank * triple_cols, triple_cols
    )
    widen_bias = lax.dynamic_slice_in_dim(
        vector_params[8 : 8 + widen_rows].reshape(-1), tensor_rank * widen_cols, widen_cols
    )
    normed, inverse = norm_stats(float_input)
    inverse = arrived([joint_gather], inverse)
    hop_all(joint_gather, *feeds)
    first_norm = (normed * first_gain + vector_params[1]).astype(jnp.bfloat16)
    second_norm = (normed * second_gain + vector_params[3]).astype(jnp.bfloat16)
    first_norm, second_norm = arrived([joint_gather, *feeds], (first_norm, second_norm))
    hop_all(joint_gather, *feeds)
    hop_all(*feeds)
    live_rows = (segment_ids >= 0).astype(jnp.float32)[:, None]
    upstream = live_rows * cotangent.astype(jnp.float32)
    upstream_low = upstream.astype(jnp.bfloat16)
    bias_grad = jnp.sum(upstream, axis=0) / tensor_size
    cosines, sines = rotary_tables(segment_ids)
    upstream_low, bias_grad, cosines, sines = arrived(
        [joint_gather, *feeds], (upstream_low, bias_grad, cosines, sines)
    )
    hop_all(*feeds)
    joint_low = placed(joint_gather.finish(), Z_ORDERS)
    attend_low, output_low = joint_low[:, :triple_cols], joint_low[:, triple_cols:]
    triple_rows = (
        jnp.einsum("dk,sd->ks", attend_low, first_norm, preferred_element_type=jnp.float32)
        + attend_bias[:, None]
    )
    mixed_rows = jnp.einsum(
        "sd,dk->ks", upstream_low, output_low, preferred_element_type=jnp.float32
    ).astype(jnp.bfloat16)
    triple_rows, mixed_rows = arrived(feeds, (triple_rows, mixed_rows))
    hop_all(*feeds)
    mixture_rows, triple_grad = attention(triple_rows, cosines, sines, mixed_rows, segment_ids)
    mixture_rows, triple_grad = arrived(feeds, (mixture_rows, triple_grad))
    output_grad = jnp.einsum(
        "sd,ks->dk", upstream_low, mixture_rows, preferred_element_type=jnp.float32
    )
    attend_grad = jnp.einsum(
        "sd,ks->dk", first_norm, triple_grad, preferred_element_type=jnp.float32
    )
    joint_scatter = Travel(
        scatter_steps(jnp.concatenate([attend_grad, output_grad], 1), X_THEN_Y)
    )
    widen_low = placed(widen_gather.finish(), widen_order)
    narrow_low = placed(narrow_gather.finish(), narrow_order)

    joint_scatter.hop()
    activated, widen_back, widen_bias_grad = feed_forward(
        second_norm, upstream_low, widen_low, narrow_low, widen_bias
    )
    activated, widen_back = arrived([joint_scatter], (activated, widen_back))
    joint_scatter.hop()
    narrow_grad = jnp.einsum(
        "sd,sf->df", upstream_low, activated, preferred_element_type=jnp.float32
    )
    widen_grad = jnp.einsum(
        "sd,sf->df", second_norm, widen_back, preferred_element_type=jnp.float32
    )
    widen_grad, narrow_grad, widen_back = arrived(
        [joint_scatter], (widen_grad, narrow_grad, widen_back)
    )
    widen_scatter = Travel(scatter_steps(widen_grad, X_THEN_Y))
    narrow_scatter = Travel(scatter_steps(narrow_grad, Y_THEN_X))
    sums = (widen_scatter, narrow_scatter)
    hop_all(*sums, joint_scatter)
    hop_all(joint_scatter)
    hop_all(joint_scatter)
    row_share = length // tensor_size
    row_start = tensor_rank * row_share
    other_row = (1 - tensor_rank) * row_share

    def core_sum(part):
        sent = lax.dynamic_slice_in_dim(part, other_row, row_share, 0).astype(jnp.bfloat16)
        kept = lax.dynamic_slice_in_dim(part, row_start, row_share, 0)
        return kept + other_core(sent).astype(jnp.float32)

    second_back = jnp.einsum("sf,df->sd", widen_back, widen_low, preferred_element_type=jnp.float32)
    first_back = jnp.einsum(
        "ks,dk->sd", triple_grad, attend_low, preferred_element_type=jnp.float32
    )
    first_total, second_total = core_sum(first_back), core_sum(second_back)
    attended = jnp.einsum(
        "ks,dk->sd", mixture_rows, output_low, preferred_element_type=jnp.float32
    )
    narrowed = jnp.einsum("sf,df->sd", activated, narrow_low, preferred_element_type=jnp.float32)
    branch_part = attended + narrowed
    column_start = tensor_rank * feature_share

    def own_columns(array):
        return lax.dynamic_slice_in_dim(array, column_start, feature_share, array.ndim - 1)

    other_start = (1 - tensor_rank) * feature_share
    branch = own_columns(branch_part) + other_core(
        lax.dynamic_slice_in_dim(branch_part, other_start, feature_share, 1)
    )
    block_output = (
        live_rows
        * (
            own_columns(float_input)
            + branch
            + own_columns(vector_params[7])
            + own_columns(vector_params[8 + widen_rows])
        )
    ).astype(jnp.bfloat16)
    attend_bias_grad = jnp.sum(triple_grad.astype(jnp.float32), axis=1)
    first_total, second_total, block_output, attend_bias_grad = arrived(
        [*sums, joint_scatter], (first_total, second_total, block_output, attend_bias_grad)
    )
    joint_sum = joint_scatter.finish()
    attend_sum, output_sum = joint_sum[:, :triple_cols], joint_sum[:, triple_cols:]
    attend_momentum = MUON_BETA * attend_moment + attend_sum
    output_momentum = MUON_BETA * output_moment + output_sum
    joint_gather = Travel(
        gather_steps(
            jnp.concatenate([attend_momentum, output_momentum], 1).astype(jnp.bfloat16), Z_ORDERS
        )
    )
    hop_all(*sums, joint_gather)
    hop_all(joint_gather)
    normed_share = lax.dynamic_slice_in_dim(normed, row_start, row_share, 0)
    inverse_share = lax.dynamic_slice_in_dim(inverse, row_start, row_share, 0)
    upstream_share = lax.dynamic_slice_in_dim(upstream, row_start, row_share, 0)
    input_share = upstream_share + (
        norm_backward(first_total, normed_share, inverse_share, first_gain)
        + norm_backward(second_total, normed_share, inverse_share, second_gain)
    )
    input_low = input_share.astype(jnp.bfloat16)
    input_other = other_core(input_low)
    input_grad = jnp.where(
        tensor_rank == 0,
        jnp.concatenate([input_low, input_other], 0),
        jnp.concatenate([input_other, input_low], 0),
    ).astype(jnp.float32)
    norm_rows = jnp.stack(
        [
            jnp.sum(first_total * normed_share, axis=0),
            jnp.sum(first_total, axis=0),
            jnp.sum(second_total * normed_share, axis=0),
            jnp.sum(second_total, axis=0),
        ]
    )
    attend_bias_full = lax.dynamic_update_slice_in_dim(
        jnp.zeros((3 * D,), jnp.float32), attend_bias_grad, tensor_rank * triple_cols, 0
    )
    widen_bias_full = lax.dynamic_update_slice_in_dim(
        jnp.zeros((FF,), jnp.float32), widen_bias_grad[0], tensor_rank * widen_cols, 0
    )
    vector_part = jnp.concatenate(
        [
            norm_rows,
            attend_bias_full.reshape(3, D),
            bias_grad[None],
            widen_bias_full.reshape(widen_rows, D),
            bias_grad[None],
        ],
        axis=0,
    )
    input_grad, vector_part = arrived([*sums, joint_gather], (input_grad, vector_part))
    vector_sum = Travel(sum_steps(vector_part))
    for _ in range(3):
        hop_all(*sums, joint_gather, vector_sum)
        arrived([*sums, joint_gather, vector_sum], ())
    widen_sum, narrow_sum = widen_scatter.finish(), narrow_scatter.finish()
    widen_momentum = MUON_BETA * widen_moment + widen_sum
    narrow_momentum = MUON_BETA * narrow_moment + narrow_sum
    widen_gather = Travel(gather_steps(widen_momentum.astype(jnp.bfloat16), widen_order))
    narrow_gather = Travel(gather_steps(narrow_momentum.astype(jnp.bfloat16), narrow_order))
    feeds = (widen_gather, narrow_gather)
    hop_all(*feeds, vector_sum)

    def gram(matrix):
        return jnp.einsum("dk,ek->de", matrix, matrix, preferred_element_type=jnp.float32)

    joint_whole = placed(joint_gather.finish(), Z_ORDERS)
    attend_whole, output_whole = joint_whole[:, :triple_cols], joint_whole[:, triple_cols:]
    attend_gram, output_gram = gram(attend_whole), gram(output_whole)
    attend_gram, output_gram = arrived([*feeds, vector_sum], (attend_gram, output_gram))
    hop_all(*feeds, vector_sum)
    arrived([*feeds, vector_sum], ())
    hop_all(*feeds)
    vector_grad = arrived(feeds, vector_sum.finish())
    hop_all(*feeds)
    arrived(feeds, ())
    hop_all(*feeds)
    widen_whole = placed(widen_gather.finish(), widen_order)
    narrow_whole = placed(narrow_gather.finish(), narrow_order)
    grams = (attend_gram, output_gram, gram(widen_whole), gram(narrow_whole))
    summed = (attend_sum, output_sum, widen_sum, narrow_sum)
    momenta = (attend_momentum, output_momentum, widen_momentum, narrow_momentum)
    widths = [matrix.shape[1] for matrix in momenta]
    rows_here = D // data_size
    wholes = (attend_whole, output_whole, widen_whole, narrow_whole)
    parity = data_rank % 2
    even, low_core = parity == 0, tensor_rank == 0
    core_first = jnp.where(even, grams[2], grams[0])
    core_second = jnp.where(even, grams[3], grams[1])
    pair_rows = newton_rows(
        jnp.where(low_core, core_first, core_second),
        other_core(jnp.where(low_core, core_second, core_first)),
        (data_rank - parity) * rows_here,
        2 * rows_here,
    )

    def rows_for(chip_parity):
        return lax.dynamic_slice_in_dim(pair_rows, chip_parity * rows_here, rows_here, 0)

    own_rows, near_rows = rows_for(parity), rows_for(1 - parity)
    devices = data_size * tensor_size

    def swapped(value, flip):
        pairs = [(index, index ^ flip) for index in range(devices)]
        return lax.ppermute(value, ("dp", "tensor"), pairs)

    core_rows, chip_rows, both_rows = (
        swapped(own_rows, 1),
        swapped(near_rows, tensor_size),
        swapped(near_rows, tensor_size + 1),
    )

    def pick(low, high):
        return jnp.where(low_core, low, high)

    here = (pick(own_rows, core_rows), pick(core_rows, own_rows))
    there = (pick(chip_rows, both_rows), pick(both_rows, chip_rows))
    ortho_rows = (
        jnp.where(even, there[0], here[0]),
        jnp.where(even, there[1], here[1]),
        jnp.where(even, here[0], there[0]),
        jnp.where(even, here[1], there[1]),
    )
    updated = []
    for matrix_index in range(4):
        longest = max(D, widths[matrix_index] * tensor_size)
        updated.append(
            masters[matrix_index] * (1.0 - MUON_RATE * MUON_DECAY)
            - MUON_RATE
            * math.sqrt(longest)
            * rows_product(ortho_rows[matrix_index], wholes[matrix_index])
        )
    first_new = BETA_ONE * vector_first + (1.0 - BETA_ONE) * vector_grad
    second_new = BETA_TWO * vector_second + (1.0 - BETA_TWO) * vector_grad * vector_grad
    first_hat = first_new / (1.0 - BETA_ONE**STEP)
    second_hat = second_new / (1.0 - BETA_TWO**STEP)
    vectors_new = vector_params - ADAM_RATE * first_hat / (jnp.sqrt(second_hat) + ADAM_EPS)
    return (
        block_output,
        input_grad,
        attend_sum,
        output_sum,
        widen_sum,
        narrow_sum,
        momenta[0],
        momenta[1],
        momenta[2],
        momenta[3],
        updated[0],
        updated[1],
        updated[2],
        updated[3],
        vector_grad,
        first_new,
        second_new,
        vectors_new,
    )


def solution(mesh):
    return jax.shard_map(
        shards,
        mesh=mesh,
        in_specs=(
            P("dp", None),
            P("dp", None),
            P("dp"),
            P("dp", "tensor"),
            P("dp", "tensor"),
            P("dp", "tensor"),
            P("dp", "tensor"),
            P("dp", "tensor"),
            P("dp", "tensor"),
            P("dp", "tensor"),
            P("dp", "tensor"),
            P(),
            P(),
            P(),
        ),
        out_specs=(
            P("dp", "tensor"),
            P("dp", None),
            P("dp", "tensor"),
            P("dp", "tensor"),
            P("dp", "tensor"),
            P("dp", "tensor"),
            P("dp", "tensor"),
            P("dp", "tensor"),
            P("dp", "tensor"),
            P("dp", "tensor"),
            P("dp", "tensor"),
            P("dp", "tensor"),
            P("dp", "tensor"),
            P("dp", "tensor"),
            P(),
            P(),
            P(),
            P(),
        ),
        check_vma=False,
    )
```

```python
import functools
import math

import jax
import jax.numpy as jnp
from jax import lax
from jax.experimental import pallas as pl
from jax.experimental.pallas import tpu as pltpu
from jax.sharding import PartitionSpec as P

D = 768
HEAD_DIM = 64
FF = 3072
ROTARY = 16
HALF = ROTARY // 2
NS_STEPS = 5
STEP = 10
QUERY_TILE = 512
FEED_TILE = 512
NEWTON_TILE = 256
MEBIBYTE = 1024 * 1024
PLACE_VMEM = 8 * MEBIBYTE
ATTENTION_VMEM = 26 * MEBIBYTE
FEED_VMEM = 26 * MEBIBYTE
NEWTON_VMEM = 32 * MEBIBYTE


X_FIRST = (0, 1, 2)
Z_THEN_X = (2, 0, 1)
Z_THEN_Y = (2, 1, 0)
Z_ORDERS = (Z_THEN_X, Z_THEN_Y)
X_THEN_Y = (0, 1, 2)
Y_THEN_X = (1, 0, 2)
NORM_EPS = 1e-05
POLY_ONE = 3.4445
POLY_TWO = -4.775
POLY_THREE = 2.0315
SCALE_EPS = 1e-07
MUON_BETA = 0.9
MUON_RATE = 0.03
MUON_DECAY = 0.1
BETA_ONE = 0.9
BETA_TWO = 0.95
ADAM_RATE = 0.1
ADAM_EPS = 1e-08


DATA_AXES = {16: ((1, 2), (2, 2), (4, 4)), 128: ((1, 4), (4, 8), (32, 4))}


def data_axes(count):
    return DATA_AXES.get(count, ((1, count), (count, 1), (count, 1)))


def ring(count, stride, size, distance):
    pairs = []
    for index in range(count):
        place = (index // stride) % size
        pairs.append((index, index + ((place + distance) % size - place) * stride))
    return pairs


def gather_sources(order, count, rank):
    sources = [rank]
    for axis in order:
        stride, size = data_axes(count)[axis]
        found, owners = list(sources), sources
        for _ in range(size - 1):
            places = [(owner // stride) % size for owner in owners]
            owners = [
                owner + ((place + size - 1) % size - place) * stride
                for owner, place in zip(owners, places)
            ]
            found += owners
        sources = found
    return sources


def place_kernel(orders, counts, width, count, *refs):
    parts, whole_ref, semaphores = list(refs[:-2]), refs[-2], refs[-1]
    copies = []
    for piece, order in enumerate(orders):
        sources = gather_sources(order, count, lax.axis_index("dp"))
        columns = pl.ds(piece * width, width)
        for part in [parts.pop(0) for _ in range(counts[piece])]:
            for row in range(part.shape[0]):
                copies.append(
                    pltpu.make_async_copy(
                        part.at[row],
                        whole_ref.at[sources.pop(0), :, columns],
                        semaphores.at[len(copies)],
                    )
                )
    for copy in copies:
        copy.start()
    for copy in copies:
        copy.wait()


def gather_steps(share, orders):
    count = lax.axis_size("dp")
    width = share.shape[1] // len(orders)
    pieces = [[share[None]]]
    for stage in range(len(orders[0])):
        if stage == 1:
            pieces = [
                [part[:, :, piece * width : (piece + 1) * width] for part in pieces[0]]
                for piece in range(len(orders))
            ]
        heads, sends = [], []
        for parts, order in zip(pieces, orders):
            stride, size = data_axes(count)[order[stage]]
            heads.append(jnp.concatenate(parts, 0) if len(parts) > 1 else parts[0])
            sends.append([ring(count, stride, size, step) for step in range(1, size)])
        got = yield [(head, perm) for head, perms in zip(heads, sends) for perm in perms]
        pieces = []
        for head, perms in zip(heads, sends):
            pieces.append([head] + got[: len(perms)])
            got = got[len(perms) :]
    return pieces


def ring_gather_steps(share, orders):
    count = lax.axis_size("dp")
    width = share.shape[1] // len(orders)
    pieces = [
        [share[None, :, piece * width : (piece + 1) * width]] for piece in range(len(orders))
    ]
    plans = [
        [(axis, hop) for axis in order for hop in range(data_axes(count)[axis][1] - 1)]
        for order in orders
    ]
    moving = [None] * len(orders)
    for step in range(len(plans[0])):
        sends = []
        for piece, plan in enumerate(plans):
            axis, hop = plan[step]
            if hop == 0:
                parts = pieces[piece]
                moving[piece] = jnp.concatenate(parts, 0) if len(parts) > 1 else parts[0]
                pieces[piece] = [moving[piece]]
            sends.append((moving[piece], ring(count, *data_axes(count)[axis], 1)))
        moving = yield sends
        for parts, part in zip(pieces, moving):
            parts.append(part)
    return pieces


def ring_scatter_steps(partial, order):
    count = lax.axis_size("dp")
    rank = lax.axis_index("dp")
    axes = data_axes(count)
    rows, columns = partial.shape[0] // count, partial.shape[1]
    slow_first = sorted(range(len(axes)), key=lambda axis: -axes[axis][0])
    held = partial.reshape(*[axes[axis][1] for axis in slow_first], rows, columns)
    for axis in order:
        stride, size = axes[axis]
        if size == 1:
            continue
        place = (rank // stride) % size
        dim = slow_first.index(axis)

        def block(target):
            return lax.dynamic_slice_in_dim(held, target % size, 1, dim)

        total = block(place + size - 1)
        for step in range(size - 1):
            (got,) = yield [(total.astype(jnp.bfloat16), ring(count, stride, size, 1))]
            total = block(place + 2 * size - 2 - step) + got.astype(jnp.float32)
        held = total
    return held.reshape(rows, columns)


class Travel:
    def __init__(self, steps):
        self.steps = steps
        self.moving = None
        self.perms = []
        self.result = None

    def load(self):
        if self.result is not None:
            return
        try:
            sends = self.steps.send(self.moving)
            self.moving = [value for value, _ in sends]
            self.perms = [perm for _, perm in sends]
        except StopIteration as stop:
            self.moving, self.perms = [], []
            self.result = stop.value

    def send(self):
        self.moving = [
            lax.ppermute(value, "dp", perm) for value, perm in zip(self.moving, self.perms)
        ]

    def hop(self):
        self.load()
        self.send()

    def finish(self):
        while True:
            self.load()
            if self.result is not None:
                return self.result
            self.send()


def joined(travels, beside):
    moving, beside = lax.optimization_barrier(([travel.moving for travel in travels], beside))
    for travel, value in zip(travels, moving):
        travel.moving = value
    return beside


def depart(travels, beside=()):
    for travel in travels:
        travel.load()
    beside = joined(travels, beside)
    for travel in travels:
        travel.send()
    return beside


def hop_all(*travels):
    for travel in travels:
        travel.hop()


def arrive(travels, beside=()):
    return joined(travels, beside)


def placed(pieces, orders):
    count = lax.axis_size("dp")
    rows, width = pieces[0][0].shape[1:]
    dtype = pieces[0][0].dtype
    anywhere = pl.BlockSpec(memory_space=pl.ANY)
    whole = pl.pallas_call(
        functools.partial(place_kernel, orders, [len(parts) for parts in pieces], width, count),
        in_specs=[anywhere] * sum(len(parts) for parts in pieces),
        out_specs=pl.BlockSpec(memory_space=pltpu.VMEM),
        out_shape=jax.ShapeDtypeStruct((count, rows, width * len(orders)), dtype),
        scratch_shapes=[pltpu.SemaphoreType.DMA((count * len(orders),))],
        compiler_params=pltpu.CompilerParams(vmem_limit_bytes=PLACE_VMEM),
        cost_estimate=pl.CostEstimate(
            flops=0, bytes_accessed=4 * count * rows * width * len(orders), transcendentals=0
        ),
    )(*[part for parts in pieces for part in parts])
    return whole.reshape(count * rows, width * len(orders))


def other_core(value):
    return lax.ppermute(value, "tensor", [(0, 1), (1, 0)])


def sum_steps(value):
    count = lax.axis_size("dp")
    distance = 1
    while distance < count:
        (got,) = yield [(value, [(index, index ^ distance) for index in range(count)])]
        value = value + got
        distance *= 2
    return value


def rows_product(left, right):
    high = left.astype(jnp.bfloat16)
    low = (left - high.astype(jnp.float32)).astype(jnp.bfloat16)
    return jnp.dot(high, right, preferred_element_type=jnp.float32) + jnp.dot(
        low, right, preferred_element_type=jnp.float32
    )


def norm_stats(values):
    row_mean = jnp.mean(values, axis=-1, keepdims=True)
    centered = values - row_mean
    row_var = jnp.mean(centered * centered, axis=-1, keepdims=True)
    inverse = lax.rsqrt(row_var + NORM_EPS)
    return (centered * inverse, inverse)


def norm_backward(incoming, normed, inverse, gain):
    scaled = incoming * gain
    return inverse * (
        scaled
        - jnp.mean(scaled, axis=-1, keepdims=True)
        - normed * jnp.mean(scaled * normed, axis=-1, keepdims=True)
    )


def rotary_tables(segments):
    token_index = jnp.arange(segments.shape[0], dtype=jnp.int32)
    leading = jnp.sum((segments == 0).astype(jnp.int32))
    position = (token_index - jnp.where(segments == 1, leading, 0)).astype(jnp.float32)
    exponent = jnp.arange(HALF, dtype=jnp.int32).astype(jnp.float32) * (2.0 / ROTARY)
    frequency = jnp.exp(-math.log(10000.0) * exponent)
    angles = frequency[:, None] * position[None, :]
    return (jnp.cos(angles), jnp.sin(angles))


def first_slots(segments):
    leading = jnp.sum((segments == 0).astype(jnp.int32))
    live = jnp.sum((segments >= 0).astype(jnp.int32))
    return jnp.where(segments == 0, 0, jnp.where(segments == 1, leading, live))


def matmul(left, right):
    return jnp.dot(left, right, preferred_element_type=jnp.float32)


def attention_kernel(
    triple_ref, cos_ref, sin_ref, upstream_ref, first_ref, mixture_ref, grad_ref, key_acc, value_acc
):
    length = triple_ref.shape[1]
    scale = 1.0 / math.sqrt(HEAD_DIM)
    cosines, sines = cos_ref[...], sin_ref[...]

    def turned(values, sign):
        first, second = values[:HALF], values[HALF:ROTARY]
        return jnp.concatenate(
            [
                first * cosines - sign * (second * sines),
                second * cosines + sign * (first * sines),
                values[ROTARY:],
            ],
            0,
        )

    def rounded(values):
        return values.astype(jnp.bfloat16).astype(jnp.float32)

    query_rows = rounded(turned(triple_ref[:HEAD_DIM], 1.0)) * scale
    key_rows = turned(triple_ref[HEAD_DIM : 2 * HEAD_DIM], 1.0)
    value_rows = triple_ref[2 * HEAD_DIM :]
    up_rows = upstream_ref[...]
    queries = query_rows.T.astype(jnp.bfloat16)
    keys = key_rows.T.astype(jnp.bfloat16)
    values = value_rows.T.astype(jnp.bfloat16)
    ups = up_rows.astype(jnp.float32).T.astype(jnp.bfloat16)
    query_rows = query_rows.astype(jnp.bfloat16)
    key_rows = key_rows.astype(jnp.bfloat16)
    value_rows = value_rows.astype(jnp.bfloat16)
    key_acc[...] = jnp.zeros_like(key_acc)
    value_acc[...] = jnp.zeros_like(value_acc)
    query_parts = []
    for tile in range(length // QUERY_TILE):
        start, stop = tile * QUERY_TILE, (tile + 1) * QUERY_TILE
        scores = matmul(keys[:stop], query_rows[:, start:stop])
        slot = lax.broadcasted_iota(jnp.int32, (stop, QUERY_TILE), 0)
        own = lax.broadcasted_iota(jnp.int32, (QUERY_TILE, QUERY_TILE), 1)
        keep = slot >= first_ref[:, start:stop]
        square = jnp.where(
            keep[start:] & (slot[:QUERY_TILE] <= own), scores[start:], -jnp.inf
        )
        if tile:
            scores = jnp.concatenate(
                [jnp.where(keep[:start], scores[:start], -jnp.inf), square], 0
            )
        else:
            scores = square
        top = jnp.max(scores, axis=0, keepdims=True)
        exponent = jnp.exp(scores - top)
        probs = exponent * (1.0 / jnp.sum(exponent, axis=0, keepdims=True))
        probs_low = probs.astype(jnp.bfloat16)
        mixture_ref[:, start:stop] = matmul(value_rows[:, :stop], probs_low).astype(jnp.bfloat16)
        prob_grad = matmul(values[:stop], up_rows[:, start:stop])
        delta = jnp.sum(probs * prob_grad, axis=0, keepdims=True)
        score_grad = (probs * (prob_grad - delta)).astype(jnp.bfloat16)
        query_parts.append(matmul(key_rows[:, :stop], score_grad))
        key_acc[:stop] += matmul(score_grad, queries[start:stop])
        value_acc[:stop] += matmul(probs_low, ups[start:stop])
    query_grad = rounded(jnp.concatenate(query_parts, 1) * scale)
    key_grad = rounded(key_acc[...].T)
    grad_ref[:HEAD_DIM] = turned(query_grad, -1.0).astype(jnp.bfloat16)
    grad_ref[HEAD_DIM : 2 * HEAD_DIM] = turned(key_grad, -1.0).astype(jnp.bfloat16)
    grad_ref[2 * HEAD_DIM :] = value_acc[...].T.astype(jnp.bfloat16)


def attention(triple_rows, cosines, sines, up_rows, segments):
    width, length = triple_rows.shape
    heads = width // (3 * HEAD_DIM)

    def whole(rows):
        return pl.BlockSpec((rows, length), lambda head: (0, 0))

    def own(rows):
        return pl.BlockSpec((rows, length), lambda head: (head, 0))

    return pl.pallas_call(
        attention_kernel,
        grid=(heads,),
        in_specs=[own(3 * HEAD_DIM), whole(HALF), whole(HALF), own(HEAD_DIM), whole(1)],
        out_specs=[own(HEAD_DIM), own(3 * HEAD_DIM)],
        out_shape=[
            jax.ShapeDtypeStruct((heads * HEAD_DIM, length), jnp.bfloat16),
            jax.ShapeDtypeStruct((width, length), jnp.bfloat16),
        ],
        scratch_shapes=[pltpu.VMEM((length, HEAD_DIM), jnp.float32)] * 2,
        compiler_params=pltpu.CompilerParams(vmem_limit_bytes=ATTENTION_VMEM),
        cost_estimate=pl.CostEstimate(
            flops=heads * 36 * length * length * HEAD_DIM,
            bytes_accessed=width * length * 8,
            transcendentals=heads * length * length,
        ),
    )(triple_rows, cosines, sines, up_rows, first_slots(segments)[None])


def split(value):
    high = value.astype(jnp.bfloat16)
    return high, (value - high.astype(jnp.float32)).astype(jnp.bfloat16)


def newton_kernel(first_ref, second_ref, rows_ref, out_ref, square, square_parts, step, left):
    wanted = rows_ref.shape[0]
    tiles = D // NEWTON_TILE

    def store_split(ref, rows, columns, value):
        high, low = split(value)
        ref[0, rows, columns] = high
        ref[1, rows, columns] = low

    def product(left_ref, rows, right_ref, columns):
        left_high, left_low = left_ref[0, rows, :], left_ref[1, rows, :]
        right_high, right_low = right_ref[0, :, columns], right_ref[1, :, columns]
        return matmul(left_high, right_high) + (
            matmul(left_high, right_low) + matmul(left_low, right_high)
        )

    def part(tile):
        return slice(tile * NEWTON_TILE, (tile + 1) * NEWTON_TILE)

    def both(store, row, column, value):
        store(part(row), part(column), value)
        if row != column:
            store(part(column), part(row), value.T)

    def put(rows, columns, value):
        square[rows, columns] = value
        store_split(square_parts, rows, columns, value)

    def diagonal(size):
        return lax.broadcasted_iota(jnp.int32, (size, size), 0) == lax.broadcasted_iota(
            jnp.int32, (size, size), 1
        )

    whole, extra = slice(None), slice(D, D + wanted)
    gram = first_ref[...] + second_ref[...]
    trace = jnp.sum(jnp.where(diagonal(D), gram, 0.0), axis=0, keepdims=True)
    trace = jnp.sum(trace, axis=1, keepdims=True)
    factor = 1.0 / (jnp.sqrt(trace) + SCALE_EPS)
    put(whole, whole, gram * (factor * factor))
    rows_value = rows_ref[...] * factor
    store_split(left, extra, whole, rows_value)
    identity = jnp.where(diagonal(NEWTON_TILE), POLY_ONE, 0.0)
    for _ in range(NS_STEPS - 1):
        for column in range(tiles):
            top = slice(0, (column + 1) * NEWTON_TILE)
            value = POLY_TWO * square[top, part(column)] + POLY_THREE * product(
                square_parts, top, square_parts, part(column)
            )
            for row in range(column + 1):
                block = value[part(row)]
                if row == column:
                    block = block + identity
                both(functools.partial(store_split, step), row, column, block)
        for column in range(tiles):
            top = slice(0, (column + 1) * NEWTON_TILE)
            value = product(step, top, square_parts, part(column))
            for row in range(column + 1):
                both(functools.partial(store_split, left), row, column, value[part(row)])
        rows_parts = []
        for column in range(tiles):
            top = slice(0, (column + 1) * NEWTON_TILE)
            value = product(left, top, step, part(column))
            rows_parts.append(product(left, extra, step, part(column)))
            for row in range(column + 1):
                both(put, row, column, value[part(row)])
        rows_value = jnp.concatenate(rows_parts, 1)
        store_split(left, extra, whole, rows_value)

    def by_square():
        return jnp.concatenate(
            [product(left, extra, square_parts, part(column)) for column in range(tiles)], 1
        )

    once = by_square()
    store_split(left, extra, whole, once)
    out_ref[...] = POLY_ONE * rows_value + POLY_TWO * once + POLY_THREE * by_square()


def newton_rows(own_gram, other_gram, first_row, rows):
    wanted = -(-rows // 16) * 16
    index = lax.broadcasted_iota(jnp.int32, (wanted, D), 0)
    chosen = lax.broadcasted_iota(jnp.int32, (wanted, D), 1) == index + first_row
    rows_out = pl.pallas_call(
        newton_kernel,
        in_specs=[pl.BlockSpec(memory_space=pltpu.VMEM)] * 3,
        out_specs=pl.BlockSpec(memory_space=pltpu.VMEM),
        out_shape=jax.ShapeDtypeStruct((wanted, D), jnp.float32),
        scratch_shapes=[
            pltpu.VMEM((D, D), jnp.float32),
            pltpu.VMEM((2, D, D), jnp.bfloat16),
            pltpu.VMEM((2, D, D), jnp.bfloat16),
            pltpu.VMEM((2, D + wanted, D), jnp.bfloat16),
        ],
        compiler_params=pltpu.CompilerParams(vmem_limit_bytes=NEWTON_VMEM),
        cost_estimate=pl.CostEstimate(
            flops=(NS_STEPS - 1) * 12 * D * D * D, bytes_accessed=8 * D * D, transcendentals=0
        ),
    )(own_gram, other_gram, chosen.astype(jnp.float32))
    return rows_out[:rows]


def feed_kernel(
    norm_ref, upstream_ref, widen_ref, narrow_ref, bias_ref, activated_ref, back_ref, sum_ref
):
    widened = matmul(norm_ref[...], widen_ref[...]) + bias_ref[...]
    incoming = matmul(upstream_ref[...], narrow_ref[...])
    area = 0.5 + 0.5 * lax.erf(widened * math.sqrt(0.5))
    density = jnp.exp(widened * widened * -0.5) * (1.0 / math.sqrt(2.0 * math.pi))
    activated_ref[...] = (widened * area).astype(jnp.bfloat16)
    back = (incoming * (area + widened * density)).astype(jnp.bfloat16)
    back_ref[...] = back
    sum_ref[...] = jnp.sum(back.astype(jnp.float32), axis=0, keepdims=True)


def feed_forward(norm, upstream, weights, bias):
    length, width = norm.shape
    hidden = weights.shape[1] // 2
    tiles = hidden // FEED_TILE

    def whole():
        return pl.BlockSpec((length, width), lambda tile: (0, 0))

    def columns(rows, first=0):
        return pl.BlockSpec((rows, FEED_TILE), lambda tile: (0, tile + first))

    return pl.pallas_call(
        feed_kernel,
        grid=(tiles,),
        in_specs=[whole(), whole(), columns(width), columns(width, tiles), columns(1)],
        out_specs=[columns(length), columns(length), columns(1)],
        out_shape=[jax.ShapeDtypeStruct((length, hidden), jnp.bfloat16)] * 2
        + [jax.ShapeDtypeStruct((1, hidden), jnp.float32)],
        compiler_params=pltpu.CompilerParams(vmem_limit_bytes=FEED_VMEM),
        cost_estimate=pl.CostEstimate(
            flops=4 * length * width * hidden,
            bytes_accessed=4 * length * (width + hidden) + 4 * width * hidden,
            transcendentals=4 * length * hidden,
        ),
    )(norm, upstream, weights, weights, bias[None])


def shards(
    layer_input,
    cotangent,
    segment_ids,
    attend_weight,
    output_weight,
    widen_weight,
    narrow_weight,
    attend_moment,
    output_moment,
    widen_moment,
    narrow_moment,
    vector_params,
    vector_first,
    vector_second,
):
    tensor_size = lax.axis_size("tensor")
    tensor_rank = lax.axis_index("tensor")
    data_size = lax.axis_size("dp")
    data_rank = lax.axis_index("dp")
    masters = (attend_weight, output_weight, widen_weight, narrow_weight)
    length = layer_input.shape[0]
    triple_cols = attend_weight.shape[1]
    widen_cols = widen_weight.shape[1]
    widen_rows = FF // D
    feature_share = D // tensor_size

    joint_gather = Travel(
        gather_steps(
            jnp.concatenate([attend_weight, output_weight], 1).astype(jnp.bfloat16), Z_ORDERS
        )
    )
    layer_input, cotangent, widen_weight, narrow_weight = depart(
        [joint_gather], (layer_input, cotangent, widen_weight, narrow_weight)
    )
    feed_share = jnp.concatenate([widen_weight, narrow_weight], 1).astype(jnp.bfloat16)
    float_input = layer_input.astype(jnp.float32)
    first_gain = vector_params[0]
    second_gain = vector_params[2]
    attend_bias = lax.dynamic_slice_in_dim(
        vector_params[4:7].reshape(-1), tensor_rank * triple_cols, triple_cols
    )
    widen_bias = lax.dynamic_slice_in_dim(
        vector_params[8 : 8 + widen_rows].reshape(-1), tensor_rank * widen_cols, widen_cols
    )
    normed, inverse = norm_stats(float_input)
    inverse, feed_share = arrive([joint_gather], (inverse, feed_share))
    feed_gather = Travel(gather_steps(feed_share, Z_ORDERS))
    depart([joint_gather])
    depart([feed_gather])
    first_norm = (normed * first_gain + vector_params[1]).astype(jnp.bfloat16)
    second_norm = (normed * second_gain + vector_params[3]).astype(jnp.bfloat16)
    first_norm, second_norm, cotangent = arrive(
        [joint_gather], (first_norm, second_norm, cotangent)
    )
    cotangent, segment_ids = depart([joint_gather], (cotangent, segment_ids))
    live_rows = (segment_ids >= 0).astype(jnp.float32)[:, None]
    upstream = live_rows * cotangent.astype(jnp.float32)
    upstream_low = upstream.astype(jnp.bfloat16)
    cosines, sines = rotary_tables(segment_ids)
    upstream_low, cosines, sines = arrive(
        [joint_gather, feed_gather], (upstream_low, cosines, sines)
    )
    joint_low = placed(joint_gather.finish(), Z_ORDERS)
    (joint_low,) = depart([feed_gather], (joint_low,))
    attend_low, output_low = joint_low[:, :triple_cols], joint_low[:, triple_cols:]
    triple_rows = (
        jnp.einsum("dk,sd->ks", attend_low, first_norm, preferred_element_type=jnp.float32)
        + attend_bias[:, None]
    )
    mixed_rows = jnp.einsum(
        "sd,dk->ks", upstream_low, output_low, preferred_element_type=jnp.float32
    ).astype(jnp.bfloat16)
    triple_rows, mixed_rows = arrive([feed_gather], (triple_rows, mixed_rows))
    triple_rows, mixed_rows = depart([feed_gather], (triple_rows, mixed_rows))
    mixture_rows, triple_grad = attention(triple_rows, cosines, sines, mixed_rows, segment_ids)
    mixture_rows, triple_grad = arrive([feed_gather], (mixture_rows, triple_grad))
    output_grad = jnp.einsum(
        "sd,ks->dk", upstream_low, mixture_rows, preferred_element_type=jnp.float32
    )
    attend_grad = jnp.einsum(
        "sd,ks->dk", first_norm, triple_grad, preferred_element_type=jnp.float32
    )
    joint_scatter = Travel(
        ring_scatter_steps(jnp.concatenate([attend_grad, output_grad], 1), Z_THEN_Y)
    )

    joint_scatter.hop()
    feed_low = placed(feed_gather.finish(), Z_ORDERS)
    widen_low, narrow_low = feed_low[:, :widen_cols], feed_low[:, widen_cols:]
    activated, widen_back, widen_bias_grad = feed_forward(
        second_norm, upstream_low, feed_low, widen_bias
    )
    narrow_grad = jnp.einsum(
        "sd,sf->df", upstream_low, activated, preferred_element_type=jnp.float32
    )
    widen_grad = jnp.einsum(
        "sd,sf->df", second_norm, widen_back, preferred_element_type=jnp.float32
    )
    widen_grad, narrow_grad, widen_back, activated, mixture_rows, triple_grad = arrive(
        [joint_scatter],
        (widen_grad, narrow_grad, widen_back, activated, mixture_rows, triple_grad),
    )
    widen_scatter = Travel(ring_scatter_steps(widen_grad, X_THEN_Y))
    narrow_scatter = Travel(ring_scatter_steps(narrow_grad, Y_THEN_X))
    sums = (widen_scatter, narrow_scatter)
    hop_all(*sums, joint_scatter)
    row_share = length // tensor_size
    row_start = tensor_rank * row_share
    other_row = (1 - tensor_rank) * row_share

    def core_sum(part):
        sent = lax.dynamic_slice_in_dim(part, other_row, row_share, 0).astype(jnp.bfloat16)
        kept = lax.dynamic_slice_in_dim(part, row_start, row_share, 0)
        return kept + other_core(sent).astype(jnp.float32)

    second_back = jnp.einsum("sf,df->sd", widen_back, widen_low, preferred_element_type=jnp.float32)
    first_back = jnp.einsum(
        "ks,dk->sd", triple_grad, attend_low, preferred_element_type=jnp.float32
    )
    first_total, second_total = core_sum(first_back), core_sum(second_back)
    attended = jnp.einsum(
        "ks,dk->sd", mixture_rows, output_low, preferred_element_type=jnp.float32
    )
    narrowed = jnp.einsum("sf,df->sd", activated, narrow_low, preferred_element_type=jnp.float32)
    branch_part = attended + narrowed
    column_start = tensor_rank * feature_share

    def own_columns(array):
        return lax.dynamic_slice_in_dim(array, column_start, feature_share, array.ndim - 1)

    other_start = (1 - tensor_rank) * feature_share
    branch = own_columns(branch_part) + other_core(
        lax.dynamic_slice_in_dim(branch_part, other_start, feature_share, 1)
    )
    block_output = (
        live_rows
        * (
            own_columns(float_input)
            + branch
            + own_columns(vector_params[7])
            + own_columns(vector_params[8 + widen_rows])
        )
    ).astype(jnp.bfloat16)
    attend_bias_grad = jnp.sum(triple_grad.astype(jnp.float32), axis=1)
    bias_grad = jnp.sum(upstream, axis=0) / tensor_size
    first_total, second_total, block_output = arrive(
        [*sums, joint_scatter], (first_total, second_total, block_output)
    )
    hop_all(*sums, joint_scatter)
    normed_share = lax.dynamic_slice_in_dim(normed, row_start, row_share, 0)
    inverse_share = lax.dynamic_slice_in_dim(inverse, row_start, row_share, 0)
    upstream_share = lax.dynamic_slice_in_dim(upstream, row_start, row_share, 0)
    input_share = upstream_share + (
        norm_backward(first_total, normed_share, inverse_share, first_gain)
        + norm_backward(second_total, normed_share, inverse_share, second_gain)
    )
    input_low = input_share.astype(jnp.bfloat16)
    input_other = other_core(input_low)
    input_grad = jnp.where(
        tensor_rank == 0,
        jnp.concatenate([input_low, input_other], 0),
        jnp.concatenate([input_other, input_low], 0),
    ).astype(jnp.float32)
    norm_rows = jnp.stack(
        [
            jnp.sum(first_total * normed_share, axis=0),
            jnp.sum(first_total, axis=0),
            jnp.sum(second_total * normed_share, axis=0),
            jnp.sum(second_total, axis=0),
        ]
    )
    attend_bias_full = lax.dynamic_update_slice_in_dim(
        jnp.zeros((3 * D,), jnp.float32), attend_bias_grad, tensor_rank * triple_cols, 0
    )
    widen_bias_full = lax.dynamic_update_slice_in_dim(
        jnp.zeros((FF,), jnp.float32), widen_bias_grad[0], tensor_rank * widen_cols, 0
    )
    vector_part = jnp.concatenate(
        [
            norm_rows,
            attend_bias_full.reshape(3, D),
            bias_grad[None],
            widen_bias_full.reshape(widen_rows, D),
            bias_grad[None],
        ],
        axis=0,
    )
    input_grad, vector_part = arrive([*sums, joint_scatter], (input_grad, vector_part))
    hop_all(*sums, joint_scatter)
    vector_part = vector_part + other_core(vector_part)
    (vector_part,) = arrive([*sums, joint_scatter], (vector_part,))
    vector_sum = Travel(sum_steps(vector_part))
    hop_all(*sums, joint_scatter, vector_sum)
    arrive([*sums, joint_scatter, vector_sum])
    joint_sum = joint_scatter.finish()
    attend_sum, output_sum = joint_sum[:, :triple_cols], joint_sum[:, triple_cols:]
    attend_momentum = MUON_BETA * attend_moment + attend_sum
    output_momentum = MUON_BETA * output_moment + output_sum
    joint_gather = Travel(
        ring_gather_steps(
            jnp.concatenate([attend_momentum, output_momentum], 1).astype(jnp.bfloat16), Z_ORDERS
        )
    )
    hop_all(*sums, joint_gather, vector_sum)
    arrive([*sums, joint_gather, vector_sum])
    widen_sum, narrow_sum = widen_scatter.finish(), narrow_scatter.finish()
    widen_momentum = MUON_BETA * widen_moment + widen_sum
    narrow_momentum = MUON_BETA * narrow_moment + narrow_sum
    widen_gather = Travel(ring_gather_steps(widen_momentum.astype(jnp.bfloat16), (Z_THEN_X,)))
    narrow_gather = Travel(ring_gather_steps(narrow_momentum.astype(jnp.bfloat16), (Z_THEN_Y,)))
    feeds = (widen_gather, narrow_gather)

    def gram(matrix):
        return jnp.einsum("dk,ek->de", matrix, matrix, preferred_element_type=jnp.float32)

    for _ in range(2):
        hop_all(*feeds, joint_gather, vector_sum)
        arrive([*feeds, joint_gather, vector_sum])
    for _ in range(2):
        hop_all(*feeds, joint_gather)
        arrive([*feeds, joint_gather])
    hop_all(*feeds)
    joint_whole = placed(joint_gather.finish(), Z_ORDERS)
    attend_whole, output_whole = joint_whole[:, :triple_cols], joint_whole[:, triple_cols:]
    attend_gram, output_gram = gram(attend_whole), gram(output_whole)
    attend_gram, output_gram = arrive(feeds, (attend_gram, output_gram))
    vector_grad = vector_sum.finish()
    widen_whole = placed(widen_gather.finish(), (Z_THEN_X,))
    narrow_whole = placed(narrow_gather.finish(), (Z_THEN_Y,))
    grams = (attend_gram, output_gram, gram(widen_whole), gram(narrow_whole))
    summed = (attend_sum, output_sum, widen_sum, narrow_sum)
    momenta = (attend_momentum, output_momentum, widen_momentum, narrow_momentum)
    widths = [matrix.shape[1] for matrix in momenta]
    rows_here = D // data_size
    wholes = (attend_whole, output_whole, widen_whole, narrow_whole)
    parity = data_rank % 2
    even, low_core = parity == 0, tensor_rank == 0
    core_first = jnp.where(even, grams[2], grams[0])
    core_second = jnp.where(even, grams[3], grams[1])
    pair_rows = newton_rows(
        jnp.where(low_core, core_first, core_second),
        other_core(jnp.where(low_core, core_second, core_first)),
        (data_rank - parity) * rows_here,
        2 * rows_here,
    )

    def rows_for(chip_parity):
        return lax.dynamic_slice_in_dim(pair_rows, chip_parity * rows_here, rows_here, 0)

    own_rows, near_rows = rows_for(parity), rows_for(1 - parity)
    devices = data_size * tensor_size

    def swapped(value, flip):
        pairs = [(index, index ^ flip) for index in range(devices)]
        return lax.ppermute(value, ("dp", "tensor"), pairs)

    core_rows, chip_rows, both_rows = (
        swapped(own_rows, 1),
        swapped(near_rows, tensor_size),
        swapped(near_rows, tensor_size + 1),
    )

    def pick(low, high):
        return jnp.where(low_core, low, high)

    here = (pick(own_rows, core_rows), pick(core_rows, own_rows))
    there = (pick(chip_rows, both_rows), pick(both_rows, chip_rows))
    ortho_rows = (
        jnp.where(even, there[0], here[0]),
        jnp.where(even, there[1], here[1]),
        jnp.where(even, here[0], there[0]),
        jnp.where(even, here[1], there[1]),
    )
    updated = []
    for matrix_index in range(4):
        longest = max(D, widths[matrix_index] * tensor_size)
        updated.append(
            masters[matrix_index] * (1.0 - MUON_RATE * MUON_DECAY)
            - MUON_RATE
            * math.sqrt(longest)
            * rows_product(ortho_rows[matrix_index], wholes[matrix_index])
        )
    first_new = BETA_ONE * vector_first + (1.0 - BETA_ONE) * vector_grad
    second_new = BETA_TWO * vector_second + (1.0 - BETA_TWO) * vector_grad * vector_grad
    first_hat = first_new / (1.0 - BETA_ONE**STEP)
    second_hat = second_new / (1.0 - BETA_TWO**STEP)
    vectors_new = vector_params - ADAM_RATE * first_hat / (jnp.sqrt(second_hat) + ADAM_EPS)
    return (
        block_output,
        input_grad,
        attend_sum,
        output_sum,
        widen_sum,
        narrow_sum,
        momenta[0],
        momenta[1],
        momenta[2],
        momenta[3],
        updated[0],
        updated[1],
        updated[2],
        updated[3],
        vector_grad,
        first_new,
        second_new,
        vectors_new,
    )


def solution(mesh):
    return jax.shard_map(
        shards,
        mesh=mesh,
        in_specs=(
            P("dp", None),
            P("dp", None),
            P("dp"),
            P("dp", "tensor"),
            P("dp", "tensor"),
            P("dp", "tensor"),
            P("dp", "tensor"),
            P("dp", "tensor"),
            P("dp", "tensor"),
            P("dp", "tensor"),
            P("dp", "tensor"),
            P(),
            P(),
            P(),
        ),
        out_specs=(
            P("dp", "tensor"),
            P("dp", None),
            P("dp", "tensor"),
            P("dp", "tensor"),
            P("dp", "tensor"),
            P("dp", "tensor"),
            P("dp", "tensor"),
            P("dp", "tensor"),
            P("dp", "tensor"),
            P("dp", "tensor"),
            P("dp", "tensor"),
            P("dp", "tensor"),
            P("dp", "tensor"),
            P("dp", "tensor"),
            P(),
            P(),
            P(),
            P(),
        ),
        check_vma=False,
    )
```

```python
import functools
import math

import jax
import jax.numpy as jnp
from jax import lax
from jax.experimental import pallas as pl
from jax.experimental.pallas import tpu as pltpu
from jax.sharding import PartitionSpec as P

D = 768
HEAD_DIM = 64
FF = 3072
ROTARY = 16
HALF = ROTARY // 2
NS_STEPS = 5
STEP = 10
QUERY_TILE = 512
FEED_TILE = 512
NEWTON_TILE = 256
MEBIBYTE = 1024 * 1024
PLACE_VMEM = 8 * MEBIBYTE
ATTENTION_VMEM = 26 * MEBIBYTE
FEED_VMEM = 26 * MEBIBYTE
NEWTON_VMEM = 32 * MEBIBYTE


X_FIRST = (0, 1, 2)
Z_THEN_X = (2, 0, 1)
Z_THEN_Y = (2, 1, 0)
Z_ORDERS = (Z_THEN_X, Z_THEN_Y)
X_THEN_Y = (0, 1, 2)
Y_THEN_X = (1, 0, 2)
NORM_EPS = 1e-05
POLY_ONE = 3.4445
POLY_TWO = -4.775
POLY_THREE = 2.0315
SCALE_EPS = 1e-07
MUON_BETA = 0.9
MUON_RATE = 0.03
MUON_DECAY = 0.1
BETA_ONE = 0.9
BETA_TWO = 0.95
ADAM_RATE = 0.1
ADAM_EPS = 1e-08


DATA_AXES = {16: ((1, 2), (2, 2), (4, 4)), 128: ((1, 4), (4, 8), (32, 4))}


def data_axes(count):
    return DATA_AXES.get(count, ((1, count), (count, 1), (count, 1)))


def ring(count, stride, size, distance):
    pairs = []
    for index in range(count):
        place = (index // stride) % size
        pairs.append((index, index + ((place + distance) % size - place) * stride))
    return pairs


def gather_sources(order, count, rank):
    sources = [rank]
    for axis in order:
        stride, size = data_axes(count)[axis]
        found, owners = list(sources), sources
        for _ in range(size - 1):
            places = [(owner // stride) % size for owner in owners]
            owners = [
                owner + ((place + size - 1) % size - place) * stride
                for owner, place in zip(owners, places)
            ]
            found += owners
        sources = found
    return sources


def place_kernel(orders, counts, width, count, *refs):
    parts, whole_ref, semaphores = list(refs[:-2]), refs[-2], refs[-1]
    copies = []
    for piece, order in enumerate(orders):
        sources = gather_sources(order, count, lax.axis_index("dp"))
        columns = pl.ds(piece * width, width)
        for part in [parts.pop(0) for _ in range(counts[piece])]:
            for row in range(part.shape[0]):
                copies.append(
                    pltpu.make_async_copy(
                        part.at[row],
                        whole_ref.at[sources.pop(0), :, columns],
                        semaphores.at[len(copies)],
                    )
                )
    for copy in copies:
        copy.start()
    for copy in copies:
        copy.wait()


def gather_steps(share, orders):
    count = lax.axis_size("dp")
    width = share.shape[1] // len(orders)
    pieces = [[share[None]]]
    for stage in range(len(orders[0])):
        if stage == 1:
            pieces = [
                [part[:, :, piece * width : (piece + 1) * width] for part in pieces[0]]
                for piece in range(len(orders))
            ]
        heads, sends = [], []
        for parts, order in zip(pieces, orders):
            stride, size = data_axes(count)[order[stage]]
            heads.append(jnp.concatenate(parts, 0) if len(parts) > 1 else parts[0])
            sends.append([ring(count, stride, size, step) for step in range(1, size)])
        got = yield [(head, perm) for head, perms in zip(heads, sends) for perm in perms]
        pieces = []
        for head, perms in zip(heads, sends):
            pieces.append([head] + got[: len(perms)])
            got = got[len(perms) :]
    return pieces


def ring_gather_steps(share, orders):
    count = lax.axis_size("dp")
    width = share.shape[1] // len(orders)
    pieces = [
        [share[None, :, piece * width : (piece + 1) * width]] for piece in range(len(orders))
    ]
    plans = [
        [(axis, hop) for axis in order for hop in range(data_axes(count)[axis][1] - 1)]
        for order in orders
    ]
    moving = [None] * len(orders)
    for step in range(len(plans[0])):
        sends = []
        for piece, plan in enumerate(plans):
            axis, hop = plan[step]
            if hop == 0:
                parts = pieces[piece]
                moving[piece] = jnp.concatenate(parts, 0) if len(parts) > 1 else parts[0]
                pieces[piece] = [moving[piece]]
            sends.append((moving[piece], ring(count, *data_axes(count)[axis], 1)))
        moving = yield sends
        for parts, part in zip(pieces, moving):
            parts.append(part)
    return pieces


def ring_scatter_steps(partial, order):
    count = lax.axis_size("dp")
    rank = lax.axis_index("dp")
    axes = data_axes(count)
    rows, columns = partial.shape[0] // count, partial.shape[1]
    slow_first = sorted(range(len(axes)), key=lambda axis: -axes[axis][0])
    held = partial.reshape(*[axes[axis][1] for axis in slow_first], rows, columns)
    for axis in order:
        stride, size = axes[axis]
        if size == 1:
            continue
        place = (rank // stride) % size
        dim = slow_first.index(axis)

        def block(target):
            return lax.dynamic_slice_in_dim(held, target % size, 1, dim)

        total = block(place + size - 1)
        for step in range(size - 1):
            (got,) = yield [(total.astype(jnp.bfloat16), ring(count, stride, size, 1))]
            total = block(place + 2 * size - 2 - step) + got.astype(jnp.float32)
        held = total
    return held.reshape(rows, columns)


class Travel:
    def __init__(self, steps):
        self.steps = steps
        self.moving = None
        self.perms = []
        self.result = None

    def load(self):
        if self.result is not None:
            return
        try:
            sends = self.steps.send(self.moving)
            self.moving = [value for value, _ in sends]
            self.perms = [perm for _, perm in sends]
        except StopIteration as stop:
            self.moving, self.perms = [], []
            self.result = stop.value

    def send(self):
        self.moving = [
            lax.ppermute(value, "dp", perm) for value, perm in zip(self.moving, self.perms)
        ]

    def hop(self):
        self.load()
        self.send()

    def finish(self):
        while True:
            self.load()
            if self.result is not None:
                return self.result
            self.send()


def joined(travels, beside):
    moving, beside = lax.optimization_barrier(([travel.moving for travel in travels], beside))
    for travel, value in zip(travels, moving):
        travel.moving = value
    return beside


def depart(travels, beside=()):
    for travel in travels:
        travel.load()
    beside = joined(travels, beside)
    for travel in travels:
        travel.send()
    return beside


def hop_all(*travels):
    for travel in travels:
        travel.hop()


def arrive(travels, beside=()):
    return joined(travels, beside)


def placed(pieces, orders):
    count = lax.axis_size("dp")
    rows, width = pieces[0][0].shape[1:]
    dtype = pieces[0][0].dtype
    anywhere = pl.BlockSpec(memory_space=pl.ANY)
    whole = pl.pallas_call(
        functools.partial(place_kernel, orders, [len(parts) for parts in pieces], width, count),
        in_specs=[anywhere] * sum(len(parts) for parts in pieces),
        out_specs=pl.BlockSpec(memory_space=pltpu.VMEM),
        out_shape=jax.ShapeDtypeStruct((count, rows, width * len(orders)), dtype),
        scratch_shapes=[pltpu.SemaphoreType.DMA((count * len(orders),))],
        compiler_params=pltpu.CompilerParams(vmem_limit_bytes=PLACE_VMEM),
        cost_estimate=pl.CostEstimate(
            flops=0, bytes_accessed=4 * count * rows * width * len(orders), transcendentals=0
        ),
    )(*[part for parts in pieces for part in parts])
    return whole.reshape(count * rows, width * len(orders))


def other_core(value):
    return lax.ppermute(value, "tensor", [(0, 1), (1, 0)])


def sum_steps(value):
    count = lax.axis_size("dp")
    distance = 1
    while distance < count:
        (got,) = yield [(value, [(index, index ^ distance) for index in range(count)])]
        value = value + got
        distance *= 2
    return value


def rows_product(left, right):
    high = left.astype(jnp.bfloat16)
    low = (left - high.astype(jnp.float32)).astype(jnp.bfloat16)
    return jnp.dot(high, right, preferred_element_type=jnp.float32) + jnp.dot(
        low, right, preferred_element_type=jnp.float32
    )


def norm_stats(values):
    row_mean = jnp.mean(values, axis=-1, keepdims=True)
    centered = values - row_mean
    row_var = jnp.mean(centered * centered, axis=-1, keepdims=True)
    inverse = lax.rsqrt(row_var + NORM_EPS)
    return (centered * inverse, inverse)


def norm_backward(incoming, normed, inverse, gain):
    scaled = incoming * gain
    return inverse * (
        scaled
        - jnp.mean(scaled, axis=-1, keepdims=True)
        - normed * jnp.mean(scaled * normed, axis=-1, keepdims=True)
    )


def rotary_tables(segments):
    token_index = jnp.arange(segments.shape[0], dtype=jnp.int32)
    leading = jnp.sum((segments == 0).astype(jnp.int32))
    position = (token_index - jnp.where(segments == 1, leading, 0)).astype(jnp.float32)
    exponent = jnp.arange(HALF, dtype=jnp.int32).astype(jnp.float32) * (2.0 / ROTARY)
    frequency = jnp.exp(-math.log(10000.0) * exponent)
    angles = frequency[:, None] * position[None, :]
    return (jnp.cos(angles), jnp.sin(angles))


def first_slots(segments):
    leading = jnp.sum((segments == 0).astype(jnp.int32))
    live = jnp.sum((segments >= 0).astype(jnp.int32))
    return jnp.where(segments == 0, 0, jnp.where(segments == 1, leading, live))


def matmul(left, right):
    return jnp.dot(left, right, preferred_element_type=jnp.float32)


def attention_kernel(
    triple_ref, cos_ref, sin_ref, upstream_ref, first_ref, mixture_ref, grad_ref, key_acc, value_acc
):
    length = triple_ref.shape[1]
    scale = 1.0 / math.sqrt(HEAD_DIM)
    cosines, sines = cos_ref[...], sin_ref[...]

    def turned(values, sign):
        first, second = values[:HALF], values[HALF:ROTARY]
        return jnp.concatenate(
            [
                first * cosines - sign * (second * sines),
                second * cosines + sign * (first * sines),
                values[ROTARY:],
            ],
            0,
        )

    def rounded(values):
        return values.astype(jnp.bfloat16).astype(jnp.float32)

    query_rows = rounded(turned(triple_ref[:HEAD_DIM], 1.0)) * scale
    key_rows = turned(triple_ref[HEAD_DIM : 2 * HEAD_DIM], 1.0)
    value_rows = triple_ref[2 * HEAD_DIM :]
    up_rows = upstream_ref[...]
    queries = query_rows.T.astype(jnp.bfloat16)
    keys = key_rows.T.astype(jnp.bfloat16)
    values = value_rows.T.astype(jnp.bfloat16)
    ups = up_rows.astype(jnp.float32).T.astype(jnp.bfloat16)
    query_rows = query_rows.astype(jnp.bfloat16)
    key_rows = key_rows.astype(jnp.bfloat16)
    value_rows = value_rows.astype(jnp.bfloat16)
    key_acc[...] = jnp.zeros_like(key_acc)
    value_acc[...] = jnp.zeros_like(value_acc)
    query_parts = []
    for tile in range(length // QUERY_TILE):
        start, stop = tile * QUERY_TILE, (tile + 1) * QUERY_TILE
        scores = matmul(keys[:stop], query_rows[:, start:stop])
        slot = lax.broadcasted_iota(jnp.int32, (stop, QUERY_TILE), 0)
        own = lax.broadcasted_iota(jnp.int32, (QUERY_TILE, QUERY_TILE), 1)
        keep = slot >= first_ref[:, start:stop]
        square = jnp.where(
            keep[start:] & (slot[:QUERY_TILE] <= own), scores[start:], -jnp.inf
        )
        if tile:
            scores = jnp.concatenate(
                [jnp.where(keep[:start], scores[:start], -jnp.inf), square], 0
            )
        else:
            scores = square
        top = jnp.max(scores, axis=0, keepdims=True)
        exponent = jnp.exp(scores - top)
        probs = exponent * (1.0 / jnp.sum(exponent, axis=0, keepdims=True))
        probs_low = probs.astype(jnp.bfloat16)
        mixture_ref[:, start:stop] = matmul(value_rows[:, :stop], probs_low).astype(jnp.bfloat16)
        prob_grad = matmul(values[:stop], up_rows[:, start:stop])
        delta = jnp.sum(probs * prob_grad, axis=0, keepdims=True)
        score_grad = (probs * (prob_grad - delta)).astype(jnp.bfloat16)
        query_parts.append(matmul(key_rows[:, :stop], score_grad))
        key_acc[:stop] += matmul(score_grad, queries[start:stop])
        value_acc[:stop] += matmul(probs_low, ups[start:stop])
    query_grad = rounded(jnp.concatenate(query_parts, 1) * scale)
    key_grad = rounded(key_acc[...].T)
    grad_ref[:HEAD_DIM] = turned(query_grad, -1.0).astype(jnp.bfloat16)
    grad_ref[HEAD_DIM : 2 * HEAD_DIM] = turned(key_grad, -1.0).astype(jnp.bfloat16)
    grad_ref[2 * HEAD_DIM :] = value_acc[...].T.astype(jnp.bfloat16)


def attention(triple_rows, cosines, sines, up_rows, segments):
    width, length = triple_rows.shape
    heads = width // (3 * HEAD_DIM)

    def whole(rows):
        return pl.BlockSpec((rows, length), lambda head: (0, 0))

    def own(rows):
        return pl.BlockSpec((rows, length), lambda head: (head, 0))

    return pl.pallas_call(
        attention_kernel,
        grid=(heads,),
        in_specs=[own(3 * HEAD_DIM), whole(HALF), whole(HALF), own(HEAD_DIM), whole(1)],
        out_specs=[own(HEAD_DIM), own(3 * HEAD_DIM)],
        out_shape=[
            jax.ShapeDtypeStruct((heads * HEAD_DIM, length), jnp.bfloat16),
            jax.ShapeDtypeStruct((width, length), jnp.bfloat16),
        ],
        scratch_shapes=[pltpu.VMEM((length, HEAD_DIM), jnp.float32)] * 2,
        compiler_params=pltpu.CompilerParams(vmem_limit_bytes=ATTENTION_VMEM),
        cost_estimate=pl.CostEstimate(
            flops=heads * 36 * length * length * HEAD_DIM,
            bytes_accessed=width * length * 8,
            transcendentals=heads * length * length,
        ),
    )(triple_rows, cosines, sines, up_rows, first_slots(segments)[None])


def split(value):
    high = value.astype(jnp.bfloat16)
    return high, (value - high.astype(jnp.float32)).astype(jnp.bfloat16)


def newton_kernel(first_ref, second_ref, rows_ref, out_ref, square, square_parts, step, left):
    wanted = rows_ref.shape[0]
    tiles = D // NEWTON_TILE

    def store_split(ref, rows, columns, value):
        high, low = split(value)
        ref[0, rows, columns] = high
        ref[1, rows, columns] = low

    def product(left_ref, rows, right_ref, columns):
        left_high, left_low = left_ref[0, rows, :], left_ref[1, rows, :]
        right_high, right_low = right_ref[0, :, columns], right_ref[1, :, columns]
        return matmul(left_high, right_high) + (
            matmul(left_high, right_low) + matmul(left_low, right_high)
        )

    def part(tile):
        return slice(tile * NEWTON_TILE, (tile + 1) * NEWTON_TILE)

    def both(store, row, column, value):
        store(part(row), part(column), value)
        if row != column:
            store(part(column), part(row), value.T)

    def put(rows, columns, value):
        square[rows, columns] = value
        store_split(square_parts, rows, columns, value)

    def diagonal(size):
        return lax.broadcasted_iota(jnp.int32, (size, size), 0) == lax.broadcasted_iota(
            jnp.int32, (size, size), 1
        )

    whole, extra = slice(None), slice(D, D + wanted)
    gram = first_ref[...] + second_ref[...]
    trace = jnp.sum(jnp.where(diagonal(D), gram, 0.0), axis=0, keepdims=True)
    trace = jnp.sum(trace, axis=1, keepdims=True)
    factor = 1.0 / (jnp.sqrt(trace) + SCALE_EPS)
    put(whole, whole, gram * (factor * factor))
    rows_value = rows_ref[...] * factor
    store_split(left, extra, whole, rows_value)
    identity = jnp.where(diagonal(NEWTON_TILE), POLY_ONE, 0.0)
    for _ in range(NS_STEPS - 1):
        for column in range(tiles):
            top = slice(0, (column + 1) * NEWTON_TILE)
            value = POLY_TWO * square[top, part(column)] + POLY_THREE * product(
                square_parts, top, square_parts, part(column)
            )
            for row in range(column + 1):
                block = value[part(row)]
                if row == column:
                    block = block + identity
                both(functools.partial(store_split, step), row, column, block)
        for column in range(tiles):
            top = slice(0, (column + 1) * NEWTON_TILE)
            value = product(step, top, square_parts, part(column))
            for row in range(column + 1):
                both(functools.partial(store_split, left), row, column, value[part(row)])
        rows_parts = []
        for column in range(tiles):
            top = slice(0, (column + 1) * NEWTON_TILE)
            value = product(left, top, step, part(column))
            rows_parts.append(product(left, extra, step, part(column)))
            for row in range(column + 1):
                both(put, row, column, value[part(row)])
        rows_value = jnp.concatenate(rows_parts, 1)
        store_split(left, extra, whole, rows_value)

    def by_square():
        return jnp.concatenate(
            [product(left, extra, square_parts, part(column)) for column in range(tiles)], 1
        )

    once = by_square()
    store_split(left, extra, whole, once)
    out_ref[...] = POLY_ONE * rows_value + POLY_TWO * once + POLY_THREE * by_square()


def newton_rows(own_gram, other_gram, first_row, rows):
    wanted = -(-rows // 16) * 16
    index = lax.broadcasted_iota(jnp.int32, (wanted, D), 0)
    chosen = lax.broadcasted_iota(jnp.int32, (wanted, D), 1) == index + first_row
    rows_out = pl.pallas_call(
        newton_kernel,
        in_specs=[pl.BlockSpec(memory_space=pltpu.VMEM)] * 3,
        out_specs=pl.BlockSpec(memory_space=pltpu.VMEM),
        out_shape=jax.ShapeDtypeStruct((wanted, D), jnp.float32),
        scratch_shapes=[
            pltpu.VMEM((D, D), jnp.float32),
            pltpu.VMEM((2, D, D), jnp.bfloat16),
            pltpu.VMEM((2, D, D), jnp.bfloat16),
            pltpu.VMEM((2, D + wanted, D), jnp.bfloat16),
        ],
        compiler_params=pltpu.CompilerParams(vmem_limit_bytes=NEWTON_VMEM),
        cost_estimate=pl.CostEstimate(
            flops=(NS_STEPS - 1) * 12 * D * D * D, bytes_accessed=8 * D * D, transcendentals=0
        ),
    )(own_gram, other_gram, chosen.astype(jnp.float32))
    return rows_out[:rows]


def feed_kernel(
    norm_ref, upstream_ref, widen_ref, narrow_ref, bias_ref, activated_ref, back_ref, sum_ref
):
    widened = matmul(norm_ref[...], widen_ref[...]) + bias_ref[...]
    incoming = matmul(upstream_ref[...], narrow_ref[...])
    area = 0.5 + 0.5 * lax.erf(widened * math.sqrt(0.5))
    density = jnp.exp(widened * widened * -0.5) * (1.0 / math.sqrt(2.0 * math.pi))
    activated_ref[...] = (widened * area).astype(jnp.bfloat16)
    back = (incoming * (area + widened * density)).astype(jnp.bfloat16)
    back_ref[...] = back
    sum_ref[...] = jnp.sum(back.astype(jnp.float32), axis=0, keepdims=True)


def feed_forward(norm, upstream, weights, bias):
    length, width = norm.shape
    hidden = weights.shape[1] // 2
    tiles = hidden // FEED_TILE

    def whole():
        return pl.BlockSpec((length, width), lambda tile: (0, 0))

    def columns(rows, first=0):
        return pl.BlockSpec((rows, FEED_TILE), lambda tile: (0, tile + first))

    return pl.pallas_call(
        feed_kernel,
        grid=(tiles,),
        in_specs=[whole(), whole(), columns(width), columns(width, tiles), columns(1)],
        out_specs=[columns(length), columns(length), columns(1)],
        out_shape=[jax.ShapeDtypeStruct((length, hidden), jnp.bfloat16)] * 2
        + [jax.ShapeDtypeStruct((1, hidden), jnp.float32)],
        compiler_params=pltpu.CompilerParams(vmem_limit_bytes=FEED_VMEM),
        cost_estimate=pl.CostEstimate(
            flops=4 * length * width * hidden,
            bytes_accessed=4 * length * (width + hidden) + 4 * width * hidden,
            transcendentals=4 * length * hidden,
        ),
    )(norm, upstream, weights, weights, bias[None])


def shards(
    layer_input,
    cotangent,
    segment_ids,
    attend_weight,
    output_weight,
    widen_weight,
    narrow_weight,
    attend_moment,
    output_moment,
    widen_moment,
    narrow_moment,
    vector_params,
    vector_first,
    vector_second,
):
    tensor_size = lax.axis_size("tensor")
    tensor_rank = lax.axis_index("tensor")
    data_size = lax.axis_size("dp")
    data_rank = lax.axis_index("dp")
    masters = (attend_weight, output_weight, widen_weight, narrow_weight)
    length = layer_input.shape[0]
    triple_cols = attend_weight.shape[1]
    widen_cols = widen_weight.shape[1]
    widen_rows = FF // D
    feature_share = D // tensor_size

    joint_gather = Travel(
        gather_steps(
            jnp.concatenate([attend_weight, output_weight], 1).astype(jnp.bfloat16), Z_ORDERS
        )
    )
    layer_input, cotangent, widen_weight, narrow_weight = depart(
        [joint_gather], (layer_input, cotangent, widen_weight, narrow_weight)
    )
    feed_share = jnp.concatenate([widen_weight, narrow_weight], 1).astype(jnp.bfloat16)
    float_input = layer_input.astype(jnp.float32)
    first_gain = vector_params[0]
    second_gain = vector_params[2]
    attend_bias = lax.dynamic_slice_in_dim(
        vector_params[4:7].reshape(-1), tensor_rank * triple_cols, triple_cols
    )
    widen_bias = lax.dynamic_slice_in_dim(
        vector_params[8 : 8 + widen_rows].reshape(-1), tensor_rank * widen_cols, widen_cols
    )
    normed, inverse = norm_stats(float_input)
    inverse, feed_share = arrive([joint_gather], (inverse, feed_share))
    feed_gather = Travel(gather_steps(feed_share, Z_ORDERS))
    depart([joint_gather])
    depart([feed_gather])
    first_norm = (normed * first_gain + vector_params[1]).astype(jnp.bfloat16)
    second_norm = (normed * second_gain + vector_params[3]).astype(jnp.bfloat16)
    first_norm, second_norm, cotangent = arrive(
        [joint_gather], (first_norm, second_norm, cotangent)
    )
    cotangent, segment_ids = depart([joint_gather], (cotangent, segment_ids))
    live_rows = (segment_ids >= 0).astype(jnp.float32)[:, None]
    upstream = live_rows * cotangent.astype(jnp.float32)
    upstream_low = upstream.astype(jnp.bfloat16)
    cosines, sines = rotary_tables(segment_ids)
    upstream_low, cosines, sines = arrive(
        [joint_gather, feed_gather], (upstream_low, cosines, sines)
    )
    joint_low = placed(joint_gather.finish(), Z_ORDERS)
    (joint_low,) = depart([feed_gather], (joint_low,))
    attend_low, output_low = joint_low[:, :triple_cols], joint_low[:, triple_cols:]
    triple_rows = (
        jnp.einsum("dk,sd->ks", attend_low, first_norm, preferred_element_type=jnp.float32)
        + attend_bias[:, None]
    )
    mixed_rows = jnp.einsum(
        "sd,dk->ks", upstream_low, output_low, preferred_element_type=jnp.float32
    ).astype(jnp.bfloat16)
    triple_rows, mixed_rows = arrive([feed_gather], (triple_rows, mixed_rows))
    triple_rows, mixed_rows = depart([feed_gather], (triple_rows, mixed_rows))
    mixture_rows, triple_grad = attention(triple_rows, cosines, sines, mixed_rows, segment_ids)
    mixture_rows, triple_grad = arrive([feed_gather], (mixture_rows, triple_grad))
    output_grad = jnp.einsum(
        "sd,ks->dk", upstream_low, mixture_rows, preferred_element_type=jnp.float32
    )
    attend_grad = jnp.einsum(
        "sd,ks->dk", first_norm, triple_grad, preferred_element_type=jnp.float32
    )
    joint_scatter = Travel(
        ring_scatter_steps(jnp.concatenate([attend_grad, output_grad], 1), Z_THEN_Y)
    )

    feed_low = placed(depart([joint_scatter], feed_gather.finish()), Z_ORDERS)
    widen_low, narrow_low = feed_low[:, :widen_cols], feed_low[:, widen_cols:]
    activated, widen_back, widen_bias_grad = feed_forward(
        second_norm, upstream_low, feed_low, widen_bias
    )
    narrow_grad = jnp.einsum(
        "sd,sf->df", upstream_low, activated, preferred_element_type=jnp.float32
    )
    widen_grad = jnp.einsum(
        "sd,sf->df", second_norm, widen_back, preferred_element_type=jnp.float32
    )
    widen_grad, narrow_grad, widen_back, activated, mixture_rows, triple_grad = arrive(
        [joint_scatter],
        (widen_grad, narrow_grad, widen_back, activated, mixture_rows, triple_grad),
    )
    widen_scatter = Travel(ring_scatter_steps(widen_grad, X_THEN_Y))
    narrow_scatter = Travel(ring_scatter_steps(narrow_grad, Y_THEN_X))
    sums = (widen_scatter, narrow_scatter)
    hop_all(*sums, joint_scatter)
    row_share = length // tensor_size
    row_start = tensor_rank * row_share
    other_row = (1 - tensor_rank) * row_share

    def core_sum(part):
        sent = lax.dynamic_slice_in_dim(part, other_row, row_share, 0).astype(jnp.bfloat16)
        kept = lax.dynamic_slice_in_dim(part, row_start, row_share, 0)
        return kept + other_core(sent).astype(jnp.float32)

    second_back = jnp.einsum("sf,df->sd", widen_back, widen_low, preferred_element_type=jnp.float32)
    first_back = jnp.einsum(
        "ks,dk->sd", triple_grad, attend_low, preferred_element_type=jnp.float32
    )
    first_total, second_total = core_sum(first_back), core_sum(second_back)
    attended = jnp.einsum(
        "ks,dk->sd", mixture_rows, output_low, preferred_element_type=jnp.float32
    )
    narrowed = jnp.einsum("sf,df->sd", activated, narrow_low, preferred_element_type=jnp.float32)
    branch_part = attended + narrowed
    column_start = tensor_rank * feature_share

    def own_columns(array):
        return lax.dynamic_slice_in_dim(array, column_start, feature_share, array.ndim - 1)

    other_start = (1 - tensor_rank) * feature_share
    branch = own_columns(branch_part) + other_core(
        lax.dynamic_slice_in_dim(branch_part, other_start, feature_share, 1)
    )
    block_output = (
        live_rows
        * (
            own_columns(float_input)
            + branch
            + own_columns(vector_params[7])
            + own_columns(vector_params[8 + widen_rows])
        )
    ).astype(jnp.bfloat16)
    attend_bias_grad = jnp.sum(triple_grad.astype(jnp.float32), axis=1)
    bias_grad = jnp.sum(upstream, axis=0) / tensor_size
    first_total, second_total, block_output = arrive(
        [*sums, joint_scatter], (first_total, second_total, block_output)
    )
    hop_all(*sums, joint_scatter)
    normed_share = lax.dynamic_slice_in_dim(normed, row_start, row_share, 0)
    inverse_share = lax.dynamic_slice_in_dim(inverse, row_start, row_share, 0)
    upstream_share = lax.dynamic_slice_in_dim(upstream, row_start, row_share, 0)
    input_share = upstream_share + (
        norm_backward(first_total, normed_share, inverse_share, first_gain)
        + norm_backward(second_total, normed_share, inverse_share, second_gain)
    )
    input_low = input_share.astype(jnp.bfloat16)
    input_other = other_core(input_low)
    input_grad = jnp.where(
        tensor_rank == 0,
        jnp.concatenate([input_low, input_other], 0),
        jnp.concatenate([input_other, input_low], 0),
    ).astype(jnp.float32)
    norm_rows = jnp.stack(
        [
            jnp.sum(first_total * normed_share, axis=0),
            jnp.sum(first_total, axis=0),
            jnp.sum(second_total * normed_share, axis=0),
            jnp.sum(second_total, axis=0),
        ]
    )
    attend_bias_full = lax.dynamic_update_slice_in_dim(
        jnp.zeros((3 * D,), jnp.float32), attend_bias_grad, tensor_rank * triple_cols, 0
    )
    widen_bias_full = lax.dynamic_update_slice_in_dim(
        jnp.zeros((FF,), jnp.float32), widen_bias_grad[0], tensor_rank * widen_cols, 0
    )
    vector_part = jnp.concatenate(
        [
            norm_rows,
            attend_bias_full.reshape(3, D),
            bias_grad[None],
            widen_bias_full.reshape(widen_rows, D),
            bias_grad[None],
        ],
        axis=0,
    )
    input_grad, vector_part = arrive([*sums, joint_scatter], (input_grad, vector_part))
    hop_all(*sums, joint_scatter)
    vector_part = vector_part + other_core(vector_part)
    (vector_part,) = arrive([*sums, joint_scatter], (vector_part,))
    vector_sum = Travel(sum_steps(vector_part))
    hop_all(*sums, joint_scatter, vector_sum)
    arrive([*sums, joint_scatter, vector_sum])
    joint_sum = joint_scatter.finish()
    attend_sum, output_sum = joint_sum[:, :triple_cols], joint_sum[:, triple_cols:]
    attend_momentum = MUON_BETA * attend_moment + attend_sum
    output_momentum = MUON_BETA * output_moment + output_sum
    joint_gather = Travel(
        ring_gather_steps(
            jnp.concatenate([attend_momentum, output_momentum], 1).astype(jnp.bfloat16), Z_ORDERS
        )
    )
    hop_all(*sums, joint_gather, vector_sum)
    arrive([*sums, joint_gather, vector_sum])
    widen_sum, narrow_sum = widen_scatter.finish(), narrow_scatter.finish()
    widen_momentum = MUON_BETA * widen_moment + widen_sum
    narrow_momentum = MUON_BETA * narrow_moment + narrow_sum
    widen_gather = Travel(ring_gather_steps(widen_momentum.astype(jnp.bfloat16), (Z_THEN_X,)))
    narrow_gather = Travel(ring_gather_steps(narrow_momentum.astype(jnp.bfloat16), (Z_THEN_Y,)))
    feeds = (widen_gather, narrow_gather)

    def gram(matrix):
        return jnp.einsum("dk,ek->de", matrix, matrix, preferred_element_type=jnp.float32)

    for _ in range(2):
        hop_all(*feeds, joint_gather, vector_sum)
        arrive([*feeds, joint_gather, vector_sum])
    for _ in range(2):
        hop_all(*feeds, joint_gather)
        arrive([*feeds, joint_gather])
    hop_all(*feeds)
    joint_whole = placed(joint_gather.finish(), Z_ORDERS)
    attend_whole, output_whole = joint_whole[:, :triple_cols], joint_whole[:, triple_cols:]
    attend_gram, output_gram = gram(attend_whole), gram(output_whole)
    attend_gram, output_gram = arrive(feeds, (attend_gram, output_gram))
    vector_grad = vector_sum.finish()
    widen_whole = placed(widen_gather.finish(), (Z_THEN_X,))
    narrow_whole = placed(narrow_gather.finish(), (Z_THEN_Y,))
    grams = (attend_gram, output_gram, gram(widen_whole), gram(narrow_whole))
    summed = (attend_sum, output_sum, widen_sum, narrow_sum)
    momenta = (attend_momentum, output_momentum, widen_momentum, narrow_momentum)
    widths = [matrix.shape[1] for matrix in momenta]
    rows_here = D // data_size
    wholes = (attend_whole, output_whole, widen_whole, narrow_whole)
    parity = data_rank % 2
    even, low_core = parity == 0, tensor_rank == 0
    core_first = jnp.where(even, grams[2], grams[0])
    core_second = jnp.where(even, grams[3], grams[1])
    pair_rows = newton_rows(
        jnp.where(low_core, core_first, core_second),
        other_core(jnp.where(low_core, core_second, core_first)),
        (data_rank - parity) * rows_here,
        2 * rows_here,
    )

    def rows_for(chip_parity):
        return lax.dynamic_slice_in_dim(pair_rows, chip_parity * rows_here, rows_here, 0)

    own_rows, near_rows = rows_for(parity), rows_for(1 - parity)
    devices = data_size * tensor_size

    def swapped(value, flip):
        pairs = [(index, index ^ flip) for index in range(devices)]
        return lax.ppermute(value, ("dp", "tensor"), pairs)

    core_rows, chip_rows, both_rows = (
        swapped(own_rows, 1),
        swapped(near_rows, tensor_size),
        swapped(near_rows, tensor_size + 1),
    )

    def pick(low, high):
        return jnp.where(low_core, low, high)

    here = (pick(own_rows, core_rows), pick(core_rows, own_rows))
    there = (pick(chip_rows, both_rows), pick(both_rows, chip_rows))
    ortho_rows = (
        jnp.where(even, there[0], here[0]),
        jnp.where(even, there[1], here[1]),
        jnp.where(even, here[0], there[0]),
        jnp.where(even, here[1], there[1]),
    )
    updated = []
    for matrix_index in range(4):
        longest = max(D, widths[matrix_index] * tensor_size)
        updated.append(
            masters[matrix_index] * (1.0 - MUON_RATE * MUON_DECAY)
            - MUON_RATE
            * math.sqrt(longest)
            * rows_product(ortho_rows[matrix_index], wholes[matrix_index])
        )
    first_new = BETA_ONE * vector_first + (1.0 - BETA_ONE) * vector_grad
    second_new = BETA_TWO * vector_second + (1.0 - BETA_TWO) * vector_grad * vector_grad
    first_hat = first_new / (1.0 - BETA_ONE**STEP)
    second_hat = second_new / (1.0 - BETA_TWO**STEP)
    vectors_new = vector_params - ADAM_RATE * first_hat / (jnp.sqrt(second_hat) + ADAM_EPS)
    return (
        block_output,
        input_grad,
        attend_sum,
        output_sum,
        widen_sum,
        narrow_sum,
        momenta[0],
        momenta[1],
        momenta[2],
        momenta[3],
        updated[0],
        updated[1],
        updated[2],
        updated[3],
        vector_grad,
        first_new,
        second_new,
        vectors_new,
    )


def solution(mesh):
    return jax.shard_map(
        shards,
        mesh=mesh,
        in_specs=(
            P("dp", None),
            P("dp", None),
            P("dp"),
            P("dp", "tensor"),
            P("dp", "tensor"),
            P("dp", "tensor"),
            P("dp", "tensor"),
            P("dp", "tensor"),
            P("dp", "tensor"),
            P("dp", "tensor"),
            P("dp", "tensor"),
            P(),
            P(),
            P(),
        ),
        out_specs=(
            P("dp", "tensor"),
            P("dp", None),
            P("dp", "tensor"),
            P("dp", "tensor"),
            P("dp", "tensor"),
            P("dp", "tensor"),
            P("dp", "tensor"),
            P("dp", "tensor"),
            P("dp", "tensor"),
            P("dp", "tensor"),
            P("dp", "tensor"),
            P("dp", "tensor"),
            P("dp", "tensor"),
            P("dp", "tensor"),
            P(),
            P(),
            P(),
            P(),
        ),
        check_vma=False,
    )
```
